512 devices in a mesh: section: 4 (over y_hi, core), phase: 8 (over x, y_lo), tp: 16 (over z).
Axes of the slice: x: 4, y: 4 (y_hi: 2, y_lo: 2; y = y_hi * 2 + y_lo), z: 16, core: 2. Of those that a mesh axis runs over, the one named last changes fastest.
Arguments:
- hidden_act: bfloat16 [1024, 28672], P(('section', 'phase'), 'tp'), may hold values from -6 to 6
- down_weight: bfloat16 [28672, 8192], P('tp', ('phase', 'section')), may hold values from -0.03125 to 0.03125
- residual: bfloat16 [1024, 8192], P('section', 'phase'), may hold values from -6 to 6
- head_weight: float32 [8192], P('phase'), may hold values from -0.011048543 to 0.011048543
- gain: float32 [8192], P('phase'), may hold values from 0.1 to 1.9
- behavior_policy_logprob: float32 [1024], replicated, may hold values from -6 to -0.05
- frozen_policy_logprob: float32 [1024], replicated, may hold values from -6 to -0.05
- old_values: float32 [1024], replicated, may hold values from -5 to 5
- judge_ratings: float32 [16], replicated, may hold values from -8 to 8
- lengths: int32 [16], replicated, may hold values from 1 to 192, 1024 in all
Outputs:
- total_loss: float32 [], replicated
- head_grad: float32 [8192], P('phase')
- down_projection_gradient: float32 [28672, 8192], P('tp', ('phase', 'section'))
- hidden_grad: bfloat16 [1024, 28672], P(('section', 'phase'), 'tp')
The draws below stay inside these ranges and needn't reach their ends.
Inputs may be any that keep to these rules, and one draw needn't show every extreme that they name: The 16 lengths sum to 1024; the longest is exactly 192.
All inputs are finite; a program needn't handle non-finite values.
Results may differ from the reference program's by a relative error of at most 0.0049.
Values may be sent and summed in bfloat16 or wider, within the bound.
No kernel may reach another device: no remote copies, remote signals or barrier semaphores. Data moves between devices by JAX's collectives and lax.ppermute only.
A program may use at most 64 MiB of HBM per device.

```python
import math
import jax
import jax.numpy as jnp
import numpy as np
from jax import lax

D = 8192
FF = 28672
TOKENS = 1024
RESP = 16
MOST = 192


def common_signs(key):
    picks = jax.random.randint(jax.random.fold_in(key, 101), (D,), 0, 2)
    return (2 * picks - 1).astype(jnp.float32)


def draw_head_weight(key, part):
    signs = common_signs(key)
    key = jax.random.fold_in(key, 1)
    magnitude = jnp.abs(jax.random.truncated_normal(key, -4.0, 4.0, (D,), jnp.float32))
    return (signs * magnitude * (0.25 / math.sqrt(D))).astype(jnp.float32)


def draw_residual(key, part):
    signs = common_signs(key)
    key = jax.random.fold_in(key, 2)
    noise_key, pull_key, flip_key = jax.random.split(key, 3)
    flips = (2 * jax.random.randint(flip_key, (TOKENS,), 0, 2) - 1).astype(jnp.float32)
    noise = jax.random.truncated_normal(noise_key, -4.5, 4.5, (TOKENS, D), jnp.float32)
    pull = jax.random.uniform(pull_key, (TOKENS,), jnp.float32, 0.25, 0.8)
    return (noise + (pull * flips)[:, None] * signs[None, :]).astype(jnp.bfloat16)


def block_scale(own_key, extent, cuts, low, top_value):
    loudness, own = 1.0, jax.random.fold_in(own_key, 6)
    for dim, shards_of in cuts:
        draws = jnp.exp(jax.random.uniform(jax.random.fold_in(own, dim), (shards_of,), jnp.float32, low / len(cuts), top_value / len(cuts)))
        loudness = loudness * jnp.repeat(draws, extent[dim] // shards_of).reshape([-1 if axis == dim else 1 for axis in range(len(extent))])
    return loudness


def split_up(amount, total, most, slope):
    weights = [(1 << 20) // math.isqrt(standing ** slope) + 1 for standing in range(2, amount + 1)]
    spare, holding = total - most - (amount - 1), [1] * (amount - 1)
    while spare > 0:
        candidates = [i for i in range(amount - 1) if holding[i] < most]
        pool, left = sum([weights[i] for i in candidates]), spare
        for i in candidates:
            addition = min(most - holding[i], max(1, left * weights[i] // pool), spare)
            holding[i] = holding[i] + addition
            spare = spare - addition
    return np.array([most] + holding)


def uneven_parts(rng, number_of, total, limit, lean):
    if number_of == 2:
        one = jax.random.randint(rng, (), max(1, total - limit), min(limit, total - 1) + 1)
        return jnp.stack([one, total - one])
    sizes = jnp.asarray(split_up(number_of, total, limit, lean), jnp.int32)
    couples = (number_of - 1) // 2
    donor, sink = sizes[1:1 + 2 * couples:2], sizes[2:2 + 2 * couples:2]
    margin = jnp.minimum(donor - 1, limit - sink)
    shifted = jax.random.randint(jax.random.fold_in(rng, 1), (couples,), 0, 1 << 20) % (margin + 1)
    sizes = sizes.at[1:1 + 2 * couples:2].set(donor - shifted).at[2:2 + 2 * couples:2].set(sink + shifted)
    return sizes[jax.random.permutation(jax.random.fold_in(rng, 2), number_of)]


def centred(key, shape, scale, most, cuts=(), kind=jnp.bfloat16):
    array = scale * jax.random.normal(key, shape, jnp.float32)
    if cuts:
        array = array * block_scale(key, shape, cuts, -0.22, 0.18)
    return jnp.clip(array, -most, most).astype(kind)


def setup_inputs(seed: int = 0) -> dict:
    arg_keys = jax.random.split(jax.random.key(seed), 11)
    return {
        "hidden_act": centred(arg_keys[0], (TOKENS, FF), 1.0, 6.0, ((0, 32), (1, 16))),
        "down_weight": centred(arg_keys[1], (FF, D), FF ** -0.5, 0.03125, ((0, 16), (1, 32))),
        "residual": draw_residual(jax.random.fold_in(arg_keys[10], 71), 0),
        "head_weight": draw_head_weight(jax.random.fold_in(arg_keys[10], 71), 0),
        "gain": jnp.clip(1.0 + 0.18 * jax.random.normal(arg_keys[4], (D,), jnp.float32), 0.1, 1.9),
        "behavior_policy_logprob": jnp.clip(jax.random.uniform(arg_keys[5], (TOKENS,), jnp.float32, -6.0, -0.05), -6.0, -0.05),
        "frozen_policy_logprob": jnp.clip(jax.random.uniform(arg_keys[6], (TOKENS,), jnp.float32, -6.0, -0.05), -6.0, -0.05),
        "old_values": centred(arg_keys[7], (TOKENS,), 1.0, 5.0, (), jnp.float32),
        "judge_ratings": centred(arg_keys[8], (RESP,), 2.0, 8.0, (), jnp.float32),
        "lengths": uneven_parts(arg_keys[9], RESP, TOKENS, MOST, 2).astype(jnp.int32),
    }


KL_PENALTY_SCALE = 0.1
TRACE_DECAY = 0.95
CLIP_RANGE = 0.2
EPSILON = 1e-05

def shaped_returns(behavior_policy_logprob, frozen_policy_logprob, old_values, judge_ratings, lengths):
    count = behavior_policy_logprob.shape[0]
    position = jnp.arange(count, dtype=jnp.int32)
    ends = jnp.cumsum(lengths).astype(jnp.int32)
    closes_sequence = position[:, None] == ends[None, :] - 1
    final = jnp.any(closes_sequence, axis=1)
    terminal_payoff_extra = lax.optimization_barrier(jnp.sum(jnp.where(closes_sequence, judge_ratings[None, :], jnp.zeros_like(judge_ratings)[None, :]), axis=1))
    per_position_payoff = terminal_payoff_extra - KL_PENALTY_SCALE * (behavior_policy_logprob - frozen_policy_logprob)
    following = jnp.concatenate([old_values[1:], jnp.zeros_like(old_values[:1])])
    following = jnp.where(final, jnp.zeros_like(following), following)
    delta = per_position_payoff + following - old_values
    segment = lax.optimization_barrier(jnp.sum((position[:, None] >= ends[None, :]).astype(jnp.int32), axis=1))
    gap = position[None, :] - position[:, None]
    inside = (segment[:, None] == segment[None, :]) & (gap >= 0)
    powers = jnp.power(jnp.full_like(delta[:1], TRACE_DECAY)[0], jnp.maximum(gap, 0).astype(delta.dtype))
    weights = jnp.where(inside, powers, jnp.zeros_like(powers))
    advantage = jnp.dot(weights, delta, precision=lax.Precision.HIGHEST)
    return advantage + old_values

def reference(hidden_act, down_weight, residual, head_weight, gain, behavior_policy_logprob, frozen_policy_logprob, old_values, judge_ratings, lengths):
    target_returns = shaped_returns(behavior_policy_logprob, frozen_policy_logprob, old_values, judge_ratings, lengths)
    block_out = jnp.dot(hidden_act, down_weight, preferred_element_type=jnp.float32)
    combined = residual.astype(jnp.float32) + block_out
    width = combined.shape[1]
    rinv = lax.rsqrt(lax.optimization_barrier(jnp.mean(combined * combined, axis=1)) + EPSILON)
    normed = combined * rinv[:, None]
    scale = gain * head_weight
    values = jnp.dot(normed, scale, precision=lax.Precision.HIGHEST)
    squash = jnp.tanh((values - old_values) / CLIP_RANGE)
    clipped = old_values + CLIP_RANGE * squash
    first = (values - target_returns) ** 2
    second = (clipped - target_returns) ** 2
    total_loss = 0.25 * jnp.sum(first + second)
    dvalue = 0.5 * (values - target_returns) + 0.5 * (clipped - target_returns) * (1.0 - squash * squash)
    head_grad = gain * lax.optimization_barrier(jnp.sum(normed * dvalue[:, None], axis=0))
    grad_rows = ((dvalue * rinv)[:, None] * (scale[None, :] - normed * (values / width)[:, None])).astype(jnp.bfloat16)
    down_projection_gradient = lax.dot_general(hidden_act, grad_rows, (((0,), (0,)), ((), ())), preferred_element_type=jnp.float32)
    hidden_grad = lax.dot_general(grad_rows, down_weight, (((1,), (1,)), ((), ())), preferred_element_type=jnp.float32).astype(jnp.bfloat16)
    return (total_loss, head_grad, down_projection_gradient, hidden_grad)
```

```python
import jax
import jax.numpy as jnp
from jax import lax
from jax.sharding import Mesh, PartitionSpec as P

D = 8192
KL_PENALTY_SCALE = 0.1
TRACE_DECAY = 0.95
CLIP_RANGE = 0.2
EPSILON = 1e-05

PLANE = ("yh", "x", "yl")
SWAP = [(0, 1), (1, 0)]
f32, bf16 = jnp.float32, jnp.bfloat16


def returns_of(behavior, frozen, old_values, judge_ratings, lengths, rows):
    total = behavior.shape[0]
    position = jnp.arange(total, dtype=jnp.int32)
    ends = jnp.cumsum(lengths)
    closes = position[:, None] == ends[None, :] - 1
    final = jnp.any(closes, axis=1)
    extra = jnp.sum(jnp.where(closes, judge_ratings[None, :], 0.0), axis=1)
    rewards = extra - KL_PENALTY_SCALE * (behavior - frozen)
    following = jnp.concatenate([old_values[1:], jnp.zeros_like(old_values[:1])])
    delta = rewards + jnp.where(final, 0.0, following) - old_values
    segment = jnp.sum((position[:, None] >= ends[None, :]).astype(jnp.int32), axis=1)
    row_seg = jnp.sum((rows[:, None] >= ends[None, :]).astype(jnp.int32), axis=1)
    gap = position[None, :] - rows[:, None]
    inside = (row_seg[:, None] == segment[None, :]) & (gap >= 0)
    powers = jnp.power(jnp.float32(TRACE_DECAY), jnp.maximum(gap, 0).astype(f32))
    return jnp.sum(jnp.where(inside, powers, 0.0) * delta[None, :], axis=1)


def pieces(x, count):
    out = []
    for _ in range(count):
        top = lax.reduce_precision(x, 8, 7)
        out.append(top.astype(bf16))
        x = x - top
    return out


def gather_all_to_all(x, axes, count):
    spread = jnp.broadcast_to(x[None], (count,) + x.shape)
    return lax.all_to_all(spread, axes, 0, 0, tiled=True)


def on_device(
    hidden_act,
    down_weight,
    residual,
    head_weight,
    gain,
    behavior,
    frozen,
    old_values,
    judge_ratings,
    lengths,
):
    yh, core, z = lax.axis_index("yh"), lax.axis_index("core"), lax.axis_index("z")
    spot = lax.axis_index(PLANE)
    rows_each, units = hidden_act.shape
    width = down_weight.shape[1]
    chip = 2 * width
    group = 16 * rows_each
    section_rows = 8 * rows_each

    other_weight = lax.ppermute(down_weight, "core", SWAP)
    weight = jnp.concatenate(
        [
            jnp.where(core == 0, down_weight, other_weight),
            jnp.where(core == 0, other_weight, down_weight),
        ],
        axis=1,
    )
    scale = lax.dynamic_slice_in_dim(gain * head_weight, yh * chip, chip, 0)
    own_scale = lax.dynamic_slice_in_dim(scale, core * width, width, 0)

    holder, block = z // 8, z % 8
    kept = lax.dynamic_slice_in_dim(residual, block * rows_each, rows_each, 0)
    sent = lax.dynamic_slice_in_dim(kept, (1 - yh) * chip, chip, 1)
    mine = lax.dynamic_slice_in_dim(kept, yh * chip, chip, 1)
    got = lax.ppermute(sent, "yh", SWAP)
    stream = jnp.where(yh == holder, mine, got)

    hidden = gather_all_to_all(hidden_act, PLANE, 16).reshape(group, units)
    other_hidden = lax.ppermute(hidden, "core", SWAP)

    partial = jnp.dot(hidden, weight, preferred_element_type=f32).astype(bf16)
    parts = lax.all_to_all(partial.reshape(16, rows_each, chip), "z", 0, 0, tiled=True)
    combined = (jnp.sum(parts.astype(f32), axis=0) + stream.astype(f32)).astype(bf16)
    combined = lax.all_gather(combined, "z", axis=0, tiled=True)

    left, right = combined[:, :width], combined[:, width:]
    own_columns = jnp.where(core == 0, left, right)
    other_columns = lax.ppermute(jnp.where(core == 0, right, left), "core", SWAP)

    wide = combined.astype(f32)
    square_part = jnp.sum(wide * wide, axis=1)
    product_part = jnp.sum(wide * scale[None, :], axis=1)
    back = (((1,), (1,)), ((), ()))
    scale_rows = jnp.stack(pieces(scale, 3) + [jnp.zeros_like(scale, dtype=bf16)] * 5)
    scale_back = jnp.sum(
        lax.dot_general(scale_rows, weight, back, preferred_element_type=f32), axis=0
    )
    back_part = lax.dot_general(combined, weight, back, preferred_element_type=f32).astype(bf16)
    small = pieces(square_part, 3) + pieces(product_part, 3) + pieces(scale_back, 2)
    small = jnp.concatenate(small)
    small = jnp.pad(small, (0, rows_each * 256 - small.shape[0])).reshape(rows_each, 256)
    payload = jnp.concatenate(
        [
            back_part.reshape(16, rows_each, units),
            jnp.broadcast_to(small[None], (16, rows_each, 256)),
        ],
        axis=2,
    )
    arrived = lax.all_to_all(payload, PLANE, 0, 0, tiled=True)
    back_sum = jnp.sum(arrived[:, :, :units].astype(f32), axis=0)
    small = jnp.sum(arrived[:, :, units:].astype(f32), axis=0).reshape(-1)
    cut = [small[i * group : (i + 1) * group] for i in range(6)]
    square_sum = cut[0] + cut[1] + cut[2]
    product_sum = cut[3] + cut[4] + cut[5]
    tail = small[6 * group : 6 * group + 2 * units].reshape(2, units)
    scale_back = tail[0] + tail[1]

    slot = jnp.arange(group, dtype=jnp.int32)
    token = slot + section_rows * (slot // section_rows + core)
    own_old = jnp.concatenate(
        [
            lax.dynamic_slice_in_dim(old_values, core * section_rows, section_rows, 0),
            lax.dynamic_slice_in_dim(old_values, (2 + core) * section_rows, section_rows, 0),
        ]
    )
    returns = own_old + returns_of(behavior, frozen, old_values, judge_ratings, lengths, token)
    rinv = lax.rsqrt(square_sum / D + EPSILON)
    values = rinv * product_sum
    squash = jnp.tanh((values - own_old) / CLIP_RANGE)
    clipped = own_old + CLIP_RANGE * squash
    first = (values - returns) ** 2
    second = (clipped - returns) ** 2
    loss = 0.25 * jnp.sum(first + second)
    dvalue = 0.5 * (values - returns) + 0.5 * (clipped - returns) * (1.0 - squash * squash)
    up = dvalue * rinv
    down = up * rinv * values / D

    own_up = lax.dynamic_slice_in_dim(up, spot * rows_each, rows_each, 0)
    own_down = lax.dynamic_slice_in_dim(down, spot * rows_each, rows_each, 0)
    hidden_grad = (own_up[:, None] * scale_back[None, :] - own_down[:, None] * back_sum).astype(bf16)

    head_part = jnp.sum(up[:, None] * wide, axis=0)
    packed = jnp.stack([up, down, head_part, jnp.full_like(up, loss)])
    other = lax.ppermute(packed, "core", SWAP)
    total_loss = loss + other[3, 0]
    head_chip = head_part + other[2]
    head_far = lax.ppermute(head_chip, "yh", SWAP)
    head_sum = jnp.concatenate(
        [jnp.where(yh == 0, head_chip, head_far), jnp.where(yh == 0, head_far, head_chip)]
    )
    head_grad = gain * head_sum

    def rows_of(up, down, columns):
        return (up[:, None] * own_scale[None, :] - down[:, None] * columns.astype(f32)).astype(bf16)

    over_tokens = (((0,), (0,)), ((), ()))
    weight_grad = lax.dot_general(
        hidden, rows_of(up, down, own_columns), over_tokens, preferred_element_type=f32
    ) + lax.dot_general(
        other_hidden,
        rows_of(other[0], other[1], other_columns),
        over_tokens,
        preferred_element_type=f32,
    )
    return (total_loss, head_grad, weight_grad, hidden_grad)


def solution(mesh):
    fine = Mesh(mesh.devices.reshape(2, 2, 4, 2, 16), ("yh", "core", "x", "yl", "z"))
    in_specs = (
        P(("yh", "core", "x", "yl"), "z"),
        P("z", ("x", "yl", "yh", "core")),
        P(("yh", "core"), ("x", "yl")),
        P(("x", "yl")),
        P(("x", "yl")),
        P(),
        P(),
        P(),
        P(),
        P(),
    )
    out_specs = (
        P(),
        P(("x", "yl")),
        P("z", ("x", "yl", "yh", "core")),
        P(("yh", "core", "x", "yl"), "z"),
    )
    return jax.shard_map(
        on_device, mesh=fine, in_specs=in_specs, out_specs=out_specs, check_vma=False
    )
```

```python
import jax
import jax.numpy as jnp
from jax import lax
from jax.experimental import pallas as pl
from jax.experimental.pallas import tpu as pltpu
from jax.sharding import Mesh, PartitionSpec as P

D = 8192
KL_PENALTY_SCALE = 0.1
TRACE_DECAY = 0.95
CLIP_RANGE = 0.2
EPSILON = 1e-05

PLANE = ("yh", "x", "yl")
SWAP = [(0, 1), (1, 0)]
f32, bf16 = jnp.float32, jnp.bfloat16


def returns_of(behavior, frozen, old_values, judge_ratings, lengths, rows):
    total = behavior.shape[0]
    position = jnp.arange(total, dtype=jnp.int32)
    ends = jnp.cumsum(lengths)
    closes = position[:, None] == ends[None, :] - 1
    final = jnp.any(closes, axis=1)
    extra = jnp.sum(jnp.where(closes, judge_ratings[None, :], 0.0), axis=1)
    rewards = extra - KL_PENALTY_SCALE * (behavior - frozen)
    following = jnp.concatenate([old_values[1:], jnp.zeros_like(old_values[:1])])
    delta = rewards + jnp.where(final, 0.0, following) - old_values
    segment = jnp.sum((position[:, None] >= ends[None, :]).astype(jnp.int32), axis=1)
    row_seg = jnp.sum((rows[:, None] >= ends[None, :]).astype(jnp.int32), axis=1)
    gap = position[None, :] - rows[:, None]
    inside = (row_seg[:, None] == segment[None, :]) & (gap >= 0)
    powers = jnp.power(jnp.float32(TRACE_DECAY), jnp.maximum(gap, 0).astype(f32))
    return jnp.sum(jnp.where(inside, powers, 0.0) * delta[None, :], axis=1)


def pieces(x, count):
    out = []
    for _ in range(count):
        top = lax.reduce_precision(x, 8, 7)
        out.append(top)
        x = x - top
    return out


def kernel_params():
    return pltpu.CompilerParams(vmem_limit_bytes=16 * 1024 * 1024)


NT = (((1,), (1,)), ((), ()))


def forward_kernel(half_ref, hidden_ref, own_ref, other_ref, out_ref):
    rows = hidden_ref[...].reshape(out_ref.shape[0], hidden_ref.shape[-1])
    width = own_ref.shape[1]
    for i, w_ref in enumerate((own_ref, other_ref)):
        product = jnp.dot(rows, w_ref[...], preferred_element_type=f32)
        out_ref[:, i * width : (i + 1) * width] = product.astype(out_ref.dtype)


def forward(hidden, own_weight, other_weight, half, dtype):
    count, rows, units = hidden.shape
    width = own_weight.shape[1]
    tokens = count // 2 * rows
    whole = pl.BlockSpec((units, width), lambda i, half: (0, 0))
    return pl.pallas_call(
        forward_kernel,
        grid_spec=pltpu.PrefetchScalarGridSpec(
            num_scalar_prefetch=1,
            grid=(1,),
            in_specs=[
                pl.BlockSpec((count // 2, 1, rows, units), lambda i, half: (0, half[0], 0, 0)),
                whole,
                whole,
            ],
            out_specs=pl.BlockSpec((tokens, 2 * width), lambda i, half: (0, 0)),
        ),
        out_shape=jax.ShapeDtypeStruct((tokens, 2 * width), dtype),
        compiler_params=kernel_params(),
        cost_estimate=pl.CostEstimate(
            flops=4 * tokens * units * width, bytes_accessed=4 * units * width, transcendentals=0
        ),
        name="forward",
    )(half.reshape(1), hidden.reshape(count // 2, 2, rows, units), own_weight, other_weight)


def back_kernel(combined_ref, own_ref, other_ref, scale_ref, base_ref, out_ref, rows_ref):
    step = pl.program_id(0)
    last = pl.num_programs(0) - 1
    width = own_ref.shape[1]
    peers, rows, lanes = out_ref.shape
    tail = own_ref.shape[0] - 3 * lanes

    def product(start, size):
        total = lax.dot_general(
            combined_ref[:, :width], own_ref[pl.ds(start, size), :], NT, preferred_element_type=f32
        ) + lax.dot_general(
            combined_ref[:, width:], other_ref[pl.ds(start, size), :], NT, preferred_element_type=f32
        )
        return total.astype(bf16).reshape(peers, rows, size)

    @pl.when(step < last)
    def _():
        out_ref[...] = product(pl.multiple_of(step * lanes, lanes), lanes)

    @pl.when(step == last)
    def _():
        out_ref[:, :, :tail] = product(3 * lanes, tail)
        both = combined_ref[...]
        wide = both.astype(f32)
        square = wide * wide
        top = square.astype(bf16)
        rest = (square - top.astype(f32)).astype(bf16)
        ones = jnp.ones((16, both.shape[1]), bf16)
        squares = lax.dot_general(ones, top, NT, preferred_element_type=f32)
        squares += lax.dot_general(ones, rest, NT, preferred_element_type=f32)
        products = lax.dot_general(scale_ref[...], both, NT, preferred_element_type=f32)
        place = 0
        for line in (squares[0:1], jnp.sum(products, axis=0, keepdims=True)):
            top = line.astype(bf16).astype(f32)
            for part in (top, line - top):
                for i in range(4):
                    rows_ref[place : place + 1, :] = part[:, i * 128 : (i + 1) * 128]
                    place += 1
        out_ref[:, :, tail:] = jnp.broadcast_to(base_ref[...][None], (peers, rows, lanes - tail))
        sums = rows_ref[...].astype(bf16)
        out_ref[:, 0:16, tail : tail + 128] = jnp.broadcast_to(sums[None], (peers, 16, 128))


def back(combined, own_weight, other_weight, scale_rows, base, peers):
    tokens, chip = combined.shape
    units, width = own_weight.shape
    rows, extra = base.shape
    lanes = (units + extra) // 4
    full = lambda a: pl.BlockSpec(a.shape, lambda j: (0, 0))
    return pl.pallas_call(
        back_kernel,
        grid=(4,),
        in_specs=[full(a) for a in (combined, own_weight, other_weight, scale_rows, base)],
        out_specs=pl.BlockSpec((peers, rows, lanes), lambda j: (0, 0, j)),
        out_shape=jax.ShapeDtypeStruct((peers, rows, units + extra), bf16),
        scratch_shapes=[pltpu.VMEM((16, 128), f32)],
        compiler_params=kernel_params(),
        cost_estimate=pl.CostEstimate(
            flops=4 * tokens * units * width, bytes_accessed=8 * units * width, transcendentals=0
        ),
        name="back",
    )(combined, own_weight, other_weight, scale_rows, base)


def token_kernel(spot_ref, arrived_ref, old_ref, returns_ref, combined_ref, grad_ref, pack_ref, up_ref):
    spot = spot_ref[0]
    peers, rows, lanes = arrived_ref.shape
    units = grad_ref.shape[1]

    def total(start, size):
        out = arrived_ref[0, :, start : start + size].astype(f32)
        for p in range(1, peers):
            out += arrived_ref[p, :, start : start + size].astype(f32)
        return out

    left = total(units, 128)
    right = total(units + 128, 128)
    square_sum = left[0:4] + left[4:8]
    product_sum = left[8:12] + left[12:16]
    old, returns = old_ref[...], returns_ref[...]
    rinv = lax.rsqrt(square_sum / D + EPSILON)
    values = rinv * product_sum
    squash = jnp.tanh((values - old) / CLIP_RANGE)
    clipped = old + CLIP_RANGE * squash
    first = (values - returns) ** 2
    second = (clipped - returns) ** 2
    loss = 0.25 * jnp.sum(first + second)
    dvalue = 0.5 * (values - returns) + 0.5 * (clipped - returns) * (1.0 - squash * squash)
    up = dvalue * rinv
    down = up * rinv * values / D
    pack_ref[0:4, :] = up
    pack_ref[4:8, :] = down
    pack_ref[12:16, :] = jnp.full((4, 128), loss, f32)

    up_ref[...] = jnp.zeros_like(up_ref)
    rest = up
    for i in range(3):
        top = rest.astype(bf16).astype(f32)
        rest = rest - top
        for r in range(4):
            up_ref[i : i + 1, r * 128 : (r + 1) * 128] = top[r : r + 1, :]
    head = jnp.dot(up_ref[...].astype(bf16), combined_ref[...], preferred_element_type=f32)
    head = jnp.sum(head, axis=0, keepdims=True)
    for r in range(4):
        pack_ref[8 + r : 9 + r, :] = head[:, r * 128 : (r + 1) * 128]

    which = lax.broadcasted_iota(jnp.int32, (4, 128), 0) == spot // 4
    lane = lax.broadcasted_iota(jnp.int32, (rows, 128), 1)
    sub = lax.broadcasted_iota(jnp.int32, (rows, 128), 0)
    pick = lane == sub + lax.rem(spot, 4) * rows

    def column(x):
        line = jnp.sum(jnp.where(which, x, 0.0), axis=0, keepdims=True)
        return jnp.sum(jnp.where(pick, line, 0.0), axis=1, keepdims=True)

    own_up, own_down = column(up), column(down)
    scale_back = left[16:32] + right[0:16]
    for k in range(units // 128):
        part = own_up * scale_back[k : k + 1, :] - own_down * total(k * 128, 128)
        grad_ref[:, k * 128 : (k + 1) * 128] = part.astype(bf16)


def token_terms(spot, arrived, old, returns, combined, units):
    full = lambda a: pl.BlockSpec(a.shape, lambda i, s: (0,) * a.ndim)
    grad = jax.ShapeDtypeStruct((arrived.shape[1], units), bf16)
    pack = jax.ShapeDtypeStruct((16, 128), f32)
    return pl.pallas_call(
        token_kernel,
        grid_spec=pltpu.PrefetchScalarGridSpec(
            num_scalar_prefetch=1,
            grid=(1,),
            in_specs=[full(a) for a in (arrived, old, returns, combined)],
            out_specs=[full(grad), full(pack)],
            scratch_shapes=[pltpu.VMEM((16, combined.shape[0]), f32)],
        ),
        out_shape=[grad, pack],
        compiler_params=kernel_params(),
        cost_estimate=pl.CostEstimate(
            flops=4 * arrived.size, bytes_accessed=2 * arrived.size, transcendentals=0
        ),
        name="token_terms",
    )(spot.reshape(1), arrived, old, returns, combined)


def weight_kernel(
    own_hidden_ref, other_hidden_ref, own_pack_ref, other_pack_ref, own_ref, other_ref, scale_ref,
    out_ref, rows_ref,
):
    tokens, width = own_ref.shape

    @pl.when(pl.program_id(0) == 0)
    def _():
        for s, (pack_ref, part_ref) in enumerate(
            ((own_pack_ref, own_ref), (other_pack_ref, other_ref))
        ):
            for r in range(tokens // 128):
                up = jnp.transpose(jnp.broadcast_to(pack_ref[r : r + 1, :], (128, 128)))
                down = jnp.transpose(jnp.broadcast_to(pack_ref[4 + r : 5 + r, :], (128, 128)))
                for h in range(width // 128):
                    cut = slice(h * 128, (h + 1) * 128)
                    part = part_ref[r * 128 : (r + 1) * 128, cut].astype(f32)
                    line = up * scale_ref[0:1, cut] - down * part
                    rows_ref[s * tokens + r * 128 : s * tokens + (r + 1) * 128, cut] = line.astype(bf16)

    out_ref[...] = jnp.dot(
        own_hidden_ref[...], rows_ref[:tokens, :], preferred_element_type=f32
    ) + jnp.dot(other_hidden_ref[...], rows_ref[tokens:, :], preferred_element_type=f32)


def weight_gradient(own_hidden, other_hidden, own_pack, other_pack, own, other, scale):
    units, tokens = own_hidden.shape
    width = own.shape[1]
    block = 256
    full = lambda a: pl.BlockSpec(a.shape, lambda i: (0, 0))
    strip = pl.BlockSpec((block, tokens), lambda i: (i, 0))
    return pl.pallas_call(
        weight_kernel,
        grid=(units // block,),
        in_specs=[strip, strip] + [full(a) for a in (own_pack, other_pack, own, other, scale)],
        out_specs=pl.BlockSpec((block, width), lambda i: (i, 0)),
        out_shape=jax.ShapeDtypeStruct((units, width), f32),
        scratch_shapes=[pltpu.VMEM((2 * tokens, width), bf16)],
        compiler_params=kernel_params(),
        cost_estimate=pl.CostEstimate(
            flops=4 * units * tokens * width, bytes_accessed=8 * units * width, transcendentals=0
        ),
        name="weight_gradient",
    )(own_hidden, other_hidden, own_pack, other_pack, own, other, scale)


def neighbours():
    pairs = [(z, z ^ 1) for z in range(16)]
    return pairs + [(16 + z, 16 + (z + (1 if z % 2 else -1)) % 16) for z in range(16)]


def on_device(
    hidden_act,
    down_weight,
    residual,
    head_weight,
    gain,
    behavior,
    frozen,
    old_values,
    judge_ratings,
    lengths,
):
    yh, core = lax.axis_index("yh"), lax.axis_index("core")
    parity = lax.axis_index("zl")
    z = 2 * lax.axis_index("zh") + parity
    spot = lax.axis_index(PLANE)
    rows_each, units = hidden_act.shape
    width = down_weight.shape[1]
    chip = 2 * width
    group = 16 * rows_each
    section_rows = 8 * rows_each

    spread = jnp.broadcast_to(hidden_act[None], (16, rows_each, units))
    hidden = lax.all_to_all(spread, PLANE, 0, 0, tiled=True)
    other_weight = lax.ppermute(down_weight, "core", SWAP)

    chip_scale = lax.dynamic_slice_in_dim(gain * head_weight, yh * chip, chip, 0)
    own_scale = lax.dynamic_slice_in_dim(chip_scale, core * width, width, 0)
    other_scale = lax.dynamic_slice_in_dim(chip_scale, (1 - core) * width, width, 0)
    scale = jnp.concatenate([own_scale, other_scale])

    kept = lax.dynamic_slice_in_dim(residual, z % 8 * rows_each, rows_each, 0)
    sent = lax.dynamic_slice_in_dim(kept, (1 - yh) * chip, chip, 1)
    mine = lax.dynamic_slice_in_dim(kept, yh * chip, chip, 1)
    stream = jnp.where(yh == z // 8, mine, lax.ppermute(sent, "yh", SWAP))
    left, right = stream[:, :width], stream[:, width:]
    stream = jnp.concatenate(
        [jnp.where(core == 0, left, right), jnp.where(core == 0, right, left)], axis=1
    )

    away = forward(hidden, down_weight, other_weight, 1 - parity, bf16)
    near = lax.ppermute(away, ("core", "zh", "zl"), neighbours())
    kept_half = forward(hidden, down_weight, other_weight, parity, f32)
    pair = (kept_half + near.astype(f32)).astype(bf16)
    parts = lax.all_to_all(pair.reshape(8, rows_each, chip), "zh", 0, 0, tiled=True)
    combined = (jnp.sum(parts.astype(f32), axis=0) + stream.astype(f32)).astype(bf16)
    combined = lax.all_gather(combined, ("zh", "zl"), axis=0, tiled=True)
    own_columns, other_columns = combined[:, :width], combined[:, width:]

    hidden_t = lax.optimization_barrier(jnp.transpose(hidden.reshape(group, units)))
    other_hidden_t = lax.ppermute(hidden_t, "core", SWAP)
    scale_rows = jnp.pad(jnp.stack(pieces(scale, 3)), ((0, 13), (0, 0))).astype(bf16)
    scale_back = lax.dot_general(
        scale_rows[:, :width], down_weight, NT, preferred_element_type=f32
    ) + lax.dot_general(scale_rows[:, width:], other_weight, NT, preferred_element_type=f32)
    high, low = pieces(jnp.sum(scale_back, axis=0).reshape(-1, 128), 2)
    base = jnp.concatenate(
        [jnp.pad(high, ((16, 16 - high.shape[0]), (0, 0))), jnp.pad(low, ((0, 32 - low.shape[0]), (0, 0)))],
        axis=1,
    ).astype(bf16)

    payload = back(combined, down_weight, other_weight, scale_rows, base, 16)
    arrived = lax.all_to_all(payload, PLANE, 0, 0, tiled=True)

    slot = jnp.arange(group, dtype=jnp.int32)
    token = slot + section_rows * (slot // section_rows + core)
    own_old = jnp.concatenate(
        [
            lax.dynamic_slice_in_dim(old_values, core * section_rows, section_rows, 0),
            lax.dynamic_slice_in_dim(old_values, (2 + core) * section_rows, section_rows, 0),
        ]
    )
    returns = own_old + returns_of(behavior, frozen, old_values, judge_ratings, lengths, token)
    hidden_grad, pack = token_terms(
        spot, arrived, own_old.reshape(4, 128), returns.reshape(4, 128), combined, units
    )
    other_pack = lax.ppermute(pack, "core", SWAP)
    total_loss = pack[12, 0] + other_pack[12, 0]
    own_head = pack[8:10] + other_pack[10:12]
    other_head = pack[10:12] + other_pack[8:10]
    head_chip = jnp.concatenate(
        [jnp.where(core == 0, own_head, other_head), jnp.where(core == 0, other_head, own_head)]
    )
    head_far = lax.ppermute(head_chip, "yh", SWAP)
    head_sum = jnp.concatenate(
        [jnp.where(yh == 0, head_chip, head_far), jnp.where(yh == 0, head_far, head_chip)]
    )
    head_grad = gain * head_sum.reshape(-1)

    weight_grad = weight_gradient(
        hidden_t,
        other_hidden_t,
        pack,
        other_pack,
        own_columns,
        lax.ppermute(other_columns, "core", SWAP),
        own_scale.reshape(1, -1),
    )
    return (total_loss, head_grad, weight_grad, hidden_grad)


def solution(mesh):
    axes = ("yh", "core", "x", "yl", "zh", "zl")
    fine = Mesh(mesh.devices.reshape(2, 2, 4, 2, 8, 2), axes)
    tp = ("zh", "zl")
    in_specs = (
        P(("yh", "core", "x", "yl"), tp),
        P(tp, ("x", "yl", "yh", "core")),
        P(("yh", "core"), ("x", "yl")),
        P(("x", "yl")),
        P(("x", "yl")),
        P(),
        P(),
        P(),
        P(),
        P(),
    )
    out_specs = (
        P(),
        P(("x", "yl")),
        P(tp, ("x", "yl", "yh", "core")),
        P(("yh", "core", "x", "yl"), tp),
    )
    return jax.shard_map(
        on_device, mesh=fine, in_specs=in_specs, out_specs=out_specs, check_vma=False
    )
```

```python
import jax
import jax.numpy as jnp
from jax import lax
from jax.experimental import pallas as pl
from jax.experimental.pallas import tpu as pltpu
from jax.sharding import Mesh, PartitionSpec as P

D = 8192
KL_PENALTY_SCALE = 0.1
TRACE_DECAY = 0.95
CLIP_RANGE = 0.2
EPSILON = 1e-05

PLANE = ("yh", "x", "yl")
SWAP = [(0, 1), (1, 0)]
f32, bf16 = jnp.float32, jnp.bfloat16


def returns_of(behavior, frozen, old_values, judge_ratings, lengths, rows):
    total = behavior.shape[0]
    position = jnp.arange(total, dtype=jnp.int32)
    ends = jnp.cumsum(lengths)
    closes = position[:, None] == ends[None, :] - 1
    final = jnp.any(closes, axis=1)
    extra = jnp.sum(jnp.where(closes, judge_ratings[None, :], 0.0), axis=1)
    rewards = extra - KL_PENALTY_SCALE * (behavior - frozen)
    following = jnp.concatenate([old_values[1:], jnp.zeros_like(old_values[:1])])
    delta = rewards + jnp.where(final, 0.0, following) - old_values
    segment = jnp.sum((position[:, None] >= ends[None, :]).astype(jnp.int32), axis=1)
    row_seg = jnp.sum((rows[:, None] >= ends[None, :]).astype(jnp.int32), axis=1)
    gap = position[None, :] - rows[:, None]
    inside = (row_seg[:, None] == segment[None, :]) & (gap >= 0)
    powers = jnp.power(jnp.float32(TRACE_DECAY), jnp.maximum(gap, 0).astype(f32))
    return jnp.sum(jnp.where(inside, powers, 0.0) * delta[None, :], axis=1)


def pieces(x, count):
    out = []
    for _ in range(count):
        top = lax.reduce_precision(x, 8, 7)
        out.append(top)
        x = x - top
    return out


def kernel_params():
    return pltpu.CompilerParams(vmem_limit_bytes=16 * 1024 * 1024)


NT = (((1,), (1,)), ((), ()))
TN = (((0,), (0,)), ((), ()))
INSIDE = pl.BlockSpec(memory_space=pltpu.VMEM)


def near(*arrays):
    return [pltpu.with_memory_space_constraint(a, pltpu.VMEM) for a in arrays]


def spread_kernel(in_ref, out_ref, held_ref, sem, sems):
    first = pltpu.make_async_copy(in_ref, held_ref, sem)
    first.start()
    first.wait()
    copies = [
        pltpu.make_async_copy(held_ref, out_ref.at[i], sems.at[i]) for i in range(out_ref.shape[0])
    ]
    for copy in copies:
        copy.start()
    for copy in copies:
        copy.wait()


def spread(x, count):
    return pl.pallas_call(
        spread_kernel,
        in_specs=[pl.BlockSpec(memory_space=pl.ANY)],
        out_specs=pl.BlockSpec(memory_space=pltpu.HBM),
        out_shape=pltpu.HBM((count,) + x.shape, x.dtype),
        scratch_shapes=[
            pltpu.VMEM(x.shape, x.dtype),
            pltpu.SemaphoreType.DMA,
            pltpu.SemaphoreType.DMA((count,)),
        ],
        compiler_params=kernel_params(),
        cost_estimate=pl.CostEstimate(flops=0, bytes_accessed=2 * count * x.size, transcendentals=0),
        name="spread",
    )(x)


def forward_kernel(half_ref, hidden_ref, own_ref, other_ref, out_ref):
    half = hidden_ref[:, pl.ds(half_ref[0], 1)]
    rows = half.reshape(out_ref.shape[0], hidden_ref.shape[-1])
    width = own_ref.shape[1]
    for i, w_ref in enumerate((own_ref, other_ref)):
        product = jnp.dot(rows, w_ref[...], preferred_element_type=f32)
        out_ref[:, i * width : (i + 1) * width] = product.astype(out_ref.dtype)


def forward(hidden, own_weight, other_weight, half, dtype):
    count, rows, units = hidden.shape
    width = own_weight.shape[1]
    tokens = count // 2 * rows
    return pl.pallas_call(
        forward_kernel,
        in_specs=[pl.BlockSpec(memory_space=pltpu.SMEM)] + [INSIDE] * 3,
        out_specs=INSIDE,
        out_shape=jax.ShapeDtypeStruct((tokens, 2 * width), dtype),
        compiler_params=kernel_params(),
        cost_estimate=pl.CostEstimate(
            flops=4 * tokens * units * width, bytes_accessed=4 * units * width, transcendentals=0
        ),
        name="forward",
    )(half.reshape(1), *near(hidden.reshape(count // 2, 2, rows, units), own_weight, other_weight))


def back_kernel(combined_ref, own_ref, other_ref, scale_ref, base_ref, out_ref, held_ref, rows_ref, sems):
    width = own_ref.shape[1]
    parts, peers, rows, lanes = held_ref.shape
    units = own_ref.shape[0]
    both = combined_ref[...]

    def send(j):
        target = out_ref.at[:, :, j * lanes : (j + 1) * lanes]
        return pltpu.make_async_copy(held_ref.at[j], target, sems.at[j])

    for j in range(parts):
        start = j * lanes
        size = min(lanes, units - start)
        total = lax.dot_general(
            both[:, :width], own_ref[start : start + size, :], NT, preferred_element_type=f32
        ) + lax.dot_general(
            both[:, width:], other_ref[start : start + size, :], NT, preferred_element_type=f32
        )
        held_ref[j, :, :, :size] = total.astype(bf16).reshape(peers, rows, size)
        if j == parts - 1:
            wide = both.astype(f32)
            square = wide * wide
            top = square.astype(bf16)
            rest = (square - top.astype(f32)).astype(bf16)
            ones = jnp.ones((16, both.shape[1]), bf16)
            squares = lax.dot_general(ones, top, NT, preferred_element_type=f32)
            squares += lax.dot_general(ones, rest, NT, preferred_element_type=f32)
            products = lax.dot_general(scale_ref[...], both, NT, preferred_element_type=f32)
            place = 0
            for line in (squares[0:1], jnp.sum(products, axis=0, keepdims=True)):
                top = line.astype(bf16).astype(f32)
                for part in (top, line - top):
                    for i in range(4):
                        rows_ref[place : place + 1, :] = part[:, i * 128 : (i + 1) * 128]
                        place += 1
            sums = rows_ref[...].astype(bf16)
            held_ref[j, :, :16, size:] = jnp.broadcast_to(sums[None], (peers, 16, 128))
            held_ref[j, :, 16:, size:] = jnp.broadcast_to(base_ref[...][None], (peers, rows - 16, 128))
        send(j).start()
    for j in range(parts):
        send(j).wait()


def back(combined, own_weight, other_weight, scale_rows, base, peers):
    tokens, chip = combined.shape
    units, width = own_weight.shape
    rows, lanes, parts = 32, units + 128, 3
    return pl.pallas_call(
        back_kernel,
        in_specs=[INSIDE] * 5,
        out_specs=pl.BlockSpec(memory_space=pltpu.HBM),
        out_shape=pltpu.HBM((peers, rows, lanes), bf16),
        scratch_shapes=[
            pltpu.VMEM((parts, peers, rows, lanes // parts), bf16),
            pltpu.VMEM((16, 128), f32),
            pltpu.SemaphoreType.DMA((parts,)),
        ],
        compiler_params=kernel_params(),
        cost_estimate=pl.CostEstimate(
            flops=4 * tokens * units * width, bytes_accessed=8 * units * width, transcendentals=0
        ),
        name="back",
    )(*near(combined, own_weight, other_weight), scale_rows, base)


def token_kernel(spot_ref, arrived_ref, old_ref, returns_ref, combined_ref, grad_ref, pack_ref, up_ref):
    spot = spot_ref[0]
    peers, rows, lanes = arrived_ref.shape
    units = grad_ref.shape[1]

    def total(start, size):
        out = arrived_ref[0, :, start : start + size].astype(f32)
        for p in range(1, peers):
            out += arrived_ref[p, :, start : start + size].astype(f32)
        return out

    left = total(units, 128)
    square_sum = left[0:4] + left[4:8]
    product_sum = left[8:12] + left[12:16]
    old, returns = old_ref[...], returns_ref[...]
    rinv = lax.rsqrt(square_sum / D + EPSILON)
    values = rinv * product_sum
    squash = jnp.tanh((values - old) / CLIP_RANGE)
    clipped = old + CLIP_RANGE * squash
    first = (values - returns) ** 2
    second = (clipped - returns) ** 2
    loss = 0.25 * jnp.sum(first + second)
    dvalue = 0.5 * (values - returns) + 0.5 * (clipped - returns) * (1.0 - squash * squash)
    up = dvalue * rinv
    down = up * rinv * values / D
    pack_ref[0:4, :] = up
    pack_ref[4:8, :] = down
    pack_ref[12:16, :] = jnp.full((4, 128), loss, f32)

    up_ref[...] = jnp.zeros_like(up_ref)
    rest = up
    for i in range(3):
        top = rest.astype(bf16).astype(f32)
        rest = rest - top
        for r in range(4):
            up_ref[i : i + 1, r * 128 : (r + 1) * 128] = top[r : r + 1, :]
    head = jnp.dot(up_ref[...].astype(bf16), combined_ref[...], preferred_element_type=f32)
    head = jnp.sum(head, axis=0, keepdims=True)
    for r in range(4):
        pack_ref[8 + r : 9 + r, :] = head[:, r * 128 : (r + 1) * 128]

    which = lax.broadcasted_iota(jnp.int32, (4, 128), 0) == spot // 4
    lane = lax.broadcasted_iota(jnp.int32, (rows, 128), 1)
    sub = lax.broadcasted_iota(jnp.int32, (rows, 128), 0)
    pick = lane == sub + lax.rem(spot, 4) * rows

    def column(x):
        line = jnp.sum(jnp.where(which, x, 0.0), axis=0, keepdims=True)
        return jnp.sum(jnp.where(pick, line, 0.0), axis=1, keepdims=True)

    own_up, own_down = column(up), column(down)
    scale_back = left[16:32]
    for k in range(units // 128):
        part = own_up * scale_back[k : k + 1, :] - own_down * total(k * 128, 128)
        grad_ref[:, k * 128 : (k + 1) * 128] = part.astype(bf16)


def token_terms(spot, arrived, old, returns, combined, units):
    full = lambda a: pl.BlockSpec(a.shape, lambda i, s: (0,) * a.ndim)
    grad = jax.ShapeDtypeStruct((arrived.shape[1], units), bf16)
    pack = jax.ShapeDtypeStruct((16, 128), f32)
    return pl.pallas_call(
        token_kernel,
        grid_spec=pltpu.PrefetchScalarGridSpec(
            num_scalar_prefetch=1,
            grid=(1,),
            in_specs=[INSIDE] * 4,
            out_specs=[full(grad), full(pack)],
            scratch_shapes=[pltpu.VMEM((16, combined.shape[0]), f32)],
        ),
        out_shape=[grad, pack],
        compiler_params=kernel_params(),
        cost_estimate=pl.CostEstimate(
            flops=4 * arrived.size, bytes_accessed=2 * arrived.size, transcendentals=0
        ),
        name="token_terms",
    )(spot.reshape(1), *near(arrived), old, returns, *near(combined))


def weight_kernel(
    own_hidden_ref, other_hidden_ref, own_pack_ref, other_pack_ref, own_ref, other_ref, scale_ref,
    out_ref, loss_ref, rows_ref,
):
    tokens, width = own_ref.shape

    @pl.when(pl.program_id(0) == 0)
    def _():
        loss_ref[0, 0] = jnp.max(own_pack_ref[12:13, :]) + jnp.max(other_pack_ref[12:13, :])
        packs = jnp.concatenate(
            [own_pack_ref[...], other_pack_ref[...], jnp.zeros((96, 128), f32)], axis=0
        )
        columns = jnp.transpose(packs)
        for s, part_ref in enumerate((own_ref, other_ref)):
            for r in range(tokens // 128):
                up = columns[:, 16 * s + r : 16 * s + r + 1]
                down = columns[:, 16 * s + 4 + r : 16 * s + 5 + r]
                part = part_ref[r * 128 : (r + 1) * 128, :].astype(f32)
                line = up * scale_ref[0:1, :] - down * part
                rows_ref[s * tokens + r * 128 : s * tokens + (r + 1) * 128, :] = line.astype(bf16)

    block = out_ref.shape[0]
    part = pl.ds(pl.multiple_of(pl.program_id(0) * block, block), block)
    out_ref[...] = lax.dot_general(
        own_hidden_ref[:, part], rows_ref[:tokens, :], TN, preferred_element_type=f32
    ) + lax.dot_general(
        other_hidden_ref[:, part], rows_ref[tokens:, :], TN, preferred_element_type=f32
    )


def weight_gradient(own_hidden, other_hidden, own_pack, other_pack, own, other, scale):
    tokens, units = own_hidden.shape
    width = own.shape[1]
    block = units // 2
    return pl.pallas_call(
        weight_kernel,
        grid=(units // block,),
        in_specs=[INSIDE] * 7,
        out_specs=[
            pl.BlockSpec((block, width), lambda i: (i, 0)),
            pl.BlockSpec(memory_space=pltpu.SMEM),
        ],
        out_shape=[
            jax.ShapeDtypeStruct((units, width), f32),
            jax.ShapeDtypeStruct((1, 1), f32),
        ],
        scratch_shapes=[pltpu.VMEM((2 * tokens, width), bf16)],
        compiler_params=kernel_params(),
        cost_estimate=pl.CostEstimate(
            flops=4 * units * tokens * width, bytes_accessed=8 * units * width, transcendentals=0
        ),
        name="weight_gradient",
    )(*near(own_hidden, other_hidden), own_pack, other_pack, *near(own, other), scale)


def neighbours():
    pairs = [(z, z ^ 1) for z in range(16)]
    return pairs + [(16 + z, 16 + (z + (1 if z % 2 else -1)) % 16) for z in range(16)]


def on_device(
    hidden_act,
    down_weight,
    residual,
    head_weight,
    gain,
    behavior,
    frozen,
    old_values,
    judge_ratings,
    lengths,
):
    yh, core = lax.axis_index("yh"), lax.axis_index("core")
    parity = lax.axis_index("zl")
    z = 2 * lax.axis_index("zh") + parity
    spot = lax.axis_index(PLANE)
    rows_each, units = hidden_act.shape
    width = down_weight.shape[1]
    chip = 2 * width
    group = 16 * rows_each
    section_rows = 8 * rows_each

    hidden = lax.all_to_all(spread(hidden_act, 16), PLANE, 0, 0, tiled=True)
    other_weight = lax.ppermute(down_weight, "core", SWAP)

    chip_scale = lax.dynamic_slice_in_dim(gain * head_weight, yh * chip, chip, 0)
    own_scale = lax.dynamic_slice_in_dim(chip_scale, core * width, width, 0)
    other_scale = lax.dynamic_slice_in_dim(chip_scale, (1 - core) * width, width, 0)
    scale = jnp.concatenate([own_scale, other_scale])

    kept = lax.dynamic_slice_in_dim(residual, z % 8 * rows_each, rows_each, 0)
    sent = lax.dynamic_slice_in_dim(kept, (1 - yh) * chip, chip, 1)
    mine = lax.dynamic_slice_in_dim(kept, yh * chip, chip, 1)
    stream = jnp.where(yh == z // 8, mine, lax.ppermute(sent, "yh", SWAP))
    left, right = stream[:, :width], stream[:, width:]
    stream = jnp.concatenate(
        [jnp.where(core == 0, left, right), jnp.where(core == 0, right, left)], axis=1
    )

    scale_rows = jnp.pad(jnp.stack(pieces(scale, 3)), ((0, 13), (0, 0))).astype(bf16)
    scale_back = lax.dot_general(
        scale_rows[:, :width], down_weight, NT, preferred_element_type=f32
    ) + lax.dot_general(scale_rows[:, width:], other_weight, NT, preferred_element_type=f32)
    base = jnp.sum(scale_back, axis=0).reshape(-1, 128)
    base = jnp.pad(base, ((0, 16 - base.shape[0]), (0, 0))).astype(bf16)
    slot = jnp.arange(group, dtype=jnp.int32)
    token = slot + section_rows * (slot // section_rows + core)
    own_old = jnp.concatenate(
        [
            lax.dynamic_slice_in_dim(old_values, core * section_rows, section_rows, 0),
            lax.dynamic_slice_in_dim(old_values, (2 + core) * section_rows, section_rows, 0),
        ]
    )
    returns = own_old + returns_of(behavior, frozen, old_values, judge_ratings, lengths, token)
    returns, own_old = returns.reshape(4, 128), own_old.reshape(4, 128)
    hidden, returns, own_old = lax.optimization_barrier((hidden, returns, own_old))

    away = forward(hidden, down_weight, other_weight, 1 - parity, bf16)
    met = lax.ppermute(away, ("core", "zh", "zl"), neighbours())
    kept_half = forward(hidden, down_weight, other_weight, parity, f32)
    pair = (kept_half + met.astype(f32)).astype(bf16)
    parts = lax.all_to_all(pair.reshape(8, rows_each, chip), "zh", 0, 0, tiled=True)
    combined = (jnp.sum(parts.astype(f32), axis=0) + stream.astype(f32)).astype(bf16)
    combined = lax.all_gather(combined, ("zh", "zl"), axis=0, tiled=True)
    own_columns, other_columns = combined[:, :width], combined[:, width:]

    payload = back(combined, down_weight, other_weight, scale_rows, base, 16)
    arrived = lax.all_to_all(payload, PLANE, 0, 0, tiled=True)
    far_columns = lax.ppermute(other_columns, "core", SWAP)
    hidden = hidden.reshape(group, units)
    far_hidden = lax.ppermute(hidden, "core", SWAP)
    arrived, far_columns, far_hidden = lax.optimization_barrier((arrived, far_columns, far_hidden))

    hidden_grad, pack = token_terms(spot, arrived, own_old, returns, combined, units)
    other_pack = lax.ppermute(pack, "core", SWAP)
    own_head = pack[8:10] + other_pack[10:12]
    other_head = pack[10:12] + other_pack[8:10]
    head_chip = jnp.concatenate(
        [jnp.where(core == 0, own_head, other_head), jnp.where(core == 0, other_head, own_head)]
    )
    head_far = lax.ppermute(head_chip, "yh", SWAP)
    head_sum = jnp.concatenate(
        [jnp.where(yh == 0, head_chip, head_far), jnp.where(yh == 0, head_far, head_chip)]
    )
    head_grad = gain * head_sum.reshape(-1)

    weight_grad, total_loss = weight_gradient(
        hidden, far_hidden, pack, other_pack, own_columns, far_columns, own_scale.reshape(1, -1)
    )
    return (total_loss[0, 0], head_grad, weight_grad, hidden_grad)


def solution(mesh):
    axes = ("yh", "core", "x", "yl", "zh", "zl")
    fine = Mesh(mesh.devices.reshape(2, 2, 4, 2, 8, 2), axes)
    tp = ("zh", "zl")
    in_specs = (
        P(("yh", "core", "x", "yl"), tp),
        P(tp, ("x", "yl", "yh", "core")),
        P(("yh", "core"), ("x", "yl")),
        P(("x", "yl")),
        P(("x", "yl")),
        P(),
        P(),
        P(),
        P(),
        P(),
    )
    out_specs = (
        P(),
        P(("x", "yl")),
        P(tp, ("x", "yl", "yh", "core")),
        P(("yh", "core", "x", "yl"), tp),
    )
    return jax.shard_map(
        on_device, mesh=fine, in_specs=in_specs, out_specs=out_specs, check_vma=False
    )
```

```python
import jax
import jax.numpy as jnp
from jax import lax
from jax.experimental import pallas as pl
from jax.experimental.pallas import tpu as pltpu
from jax.sharding import Mesh, PartitionSpec as P

D = 8192
KL_PENALTY_SCALE = 0.1
TRACE_DECAY = 0.95
CLIP_RANGE = 0.2
EPSILON = 1e-05

PLANE = ("yh", "x", "yl")
SWAP = [(0, 1), (1, 0)]
f32, bf16 = jnp.float32, jnp.bfloat16


def returns_of(behavior, frozen, old_values, judge_ratings, lengths, rows):
    total = behavior.shape[0]
    position = jnp.arange(total, dtype=jnp.int32)
    ends = jnp.cumsum(lengths)
    closes = position[:, None] == ends[None, :] - 1
    final = jnp.any(closes, axis=1)
    extra = jnp.sum(jnp.where(closes, judge_ratings[None, :], 0.0), axis=1)
    rewards = extra - KL_PENALTY_SCALE * (behavior - frozen)
    following = jnp.concatenate([old_values[1:], jnp.zeros_like(old_values[:1])])
    delta = rewards + jnp.where(final, 0.0, following) - old_values
    segment = jnp.sum((position[:, None] >= ends[None, :]).astype(jnp.int32), axis=1)
    row_seg = jnp.sum((rows[:, None] >= ends[None, :]).astype(jnp.int32), axis=1)
    gap = position[None, :] - rows[:, None]
    inside = (row_seg[:, None] == segment[None, :]) & (gap >= 0)
    powers = jnp.power(jnp.float32(TRACE_DECAY), jnp.maximum(gap, 0).astype(f32))
    return jnp.sum(jnp.where(inside, powers, 0.0) * delta[None, :], axis=1)


def pieces(x, count):
    out = []
    for _ in range(count):
        top = lax.reduce_precision(x, 8, 7)
        out.append(top)
        x = x - top
    return out


def kernel_params():
    return pltpu.CompilerParams(vmem_limit_bytes=16 * 1024 * 1024)


NT = (((1,), (1,)), ((), ()))
TN = (((0,), (0,)), ((), ()))
INSIDE = pl.BlockSpec(memory_space=pltpu.VMEM)
OUTSIDE = pl.BlockSpec(memory_space=pl.ANY)


def near(*arrays):
    return [pltpu.with_memory_space_constraint(a, pltpu.VMEM) for a in arrays]


def far(array):
    return pltpu.with_memory_space_constraint(array, pltpu.HBM)


def hold_kernel(in_ref, out_ref, sem):
    copy = pltpu.make_async_copy(in_ref, out_ref, sem)
    copy.start()
    copy.wait()


def hold(x):
    return pl.pallas_call(
        hold_kernel,
        in_specs=[pl.BlockSpec(memory_space=pl.ANY)],
        out_specs=INSIDE,
        out_shape=pltpu.VMEM(x.shape, x.dtype),
        scratch_shapes=[pltpu.SemaphoreType.DMA],
        compiler_params=kernel_params(),
        cost_estimate=pl.CostEstimate(flops=0, bytes_accessed=4 * x.size, transcendentals=0),
        name="hold",
    )(x)


def spread_kernel(in_ref, out_ref, held_ref, sem, sems):
    first = pltpu.make_async_copy(in_ref, held_ref, sem)
    first.start()
    first.wait()
    copies = [
        pltpu.make_async_copy(held_ref, out_ref.at[i], sems.at[i]) for i in range(out_ref.shape[0])
    ]
    for copy in copies:
        copy.start()
    for copy in copies:
        copy.wait()


def spread(x, count):
    return pl.pallas_call(
        spread_kernel,
        in_specs=[pl.BlockSpec(memory_space=pl.ANY)],
        out_specs=pl.BlockSpec(memory_space=pltpu.HBM),
        out_shape=pltpu.HBM((count,) + x.shape, x.dtype),
        scratch_shapes=[
            pltpu.VMEM(x.shape, x.dtype),
            pltpu.SemaphoreType.DMA,
            pltpu.SemaphoreType.DMA((count,)),
        ],
        compiler_params=kernel_params(),
        cost_estimate=pl.CostEstimate(flops=0, bytes_accessed=2 * count * x.size, transcendentals=0),
        name="spread",
    )(x)


def forward_kernel(half_ref, hidden_ref, own_ref, other_ref, out_ref):
    half = hidden_ref[:, pl.ds(half_ref[0], 1)]
    rows = half.reshape(out_ref.shape[0], hidden_ref.shape[-1])
    width = own_ref.shape[1]
    for i, w_ref in enumerate((own_ref, other_ref)):
        product = jnp.dot(rows, w_ref[...], preferred_element_type=f32)
        out_ref[:, i * width : (i + 1) * width] = product.astype(out_ref.dtype)


def forward(hidden, own_weight, other_weight, half, dtype):
    count, rows, units = hidden.shape
    width = own_weight.shape[1]
    tokens = count // 2 * rows
    return pl.pallas_call(
        forward_kernel,
        in_specs=[pl.BlockSpec(memory_space=pltpu.SMEM)] + [INSIDE] * 3,
        out_specs=INSIDE,
        out_shape=jax.ShapeDtypeStruct((tokens, 2 * width), dtype),
        compiler_params=kernel_params(),
        cost_estimate=pl.CostEstimate(
            flops=4 * tokens * units * width, bytes_accessed=4 * units * width, transcendentals=0
        ),
        name="forward",
    )(half.reshape(1), *near(hidden.reshape(count // 2, 2, rows, units), own_weight, other_weight))


def sums_kernel(combined_ref, scale_ref, base_ref, out_ref, held_ref, rows_ref, sem):
    peers, rows, lanes = out_ref.shape
    both = combined_ref[...]
    wide = both.astype(f32)
    square = wide * wide
    top = square.astype(bf16)
    rest = (square - top.astype(f32)).astype(bf16)
    ones = jnp.ones((16, both.shape[1]), bf16)
    squares = lax.dot_general(ones, top, NT, preferred_element_type=f32)
    squares += lax.dot_general(ones, rest, NT, preferred_element_type=f32)
    products = lax.dot_general(scale_ref[...], both, NT, preferred_element_type=f32)
    place = 0
    for line in (squares[0:1], jnp.sum(products, axis=0, keepdims=True)):
        top = line.astype(bf16).astype(f32)
        for part in (top, line - top):
            for i in range(4):
                rows_ref[place : place + 1, :] = part[:, i * lanes : (i + 1) * lanes]
                place += 1
    sums = rows_ref[...].astype(bf16)
    held_ref[:, :16, :] = jnp.broadcast_to(sums[None], (peers, 16, lanes))
    held_ref[:, 16:, :] = jnp.broadcast_to(base_ref[...][None], (peers, rows - 16, lanes))
    copy = pltpu.make_async_copy(held_ref, out_ref, sem)
    copy.start()
    copy.wait()


def token_sums(combined, scale_rows, base, peers):
    shape = (peers, 32, 128)
    return pl.pallas_call(
        sums_kernel,
        in_specs=[INSIDE] * 3,
        out_specs=pl.BlockSpec(memory_space=pltpu.HBM),
        out_shape=pltpu.HBM(shape, bf16),
        scratch_shapes=[pltpu.VMEM(shape, bf16), pltpu.VMEM((16, 128), f32), pltpu.SemaphoreType.DMA],
        compiler_params=kernel_params(),
        cost_estimate=pl.CostEstimate(flops=96 * combined.size, bytes_accessed=2 * combined.size, transcendentals=0),
        name="token_sums",
    )(*near(combined), scale_rows, base)


def back_kernel(combined_ref, outer_ref, other_ref, out_ref, own_ref, held_ref, sem, sems):
    copy = pltpu.make_async_copy(outer_ref, own_ref, sem)
    copy.start()
    width = own_ref.shape[1]
    parts, peers, rows, lanes = held_ref.shape

    def send(j):
        target = out_ref.at[:, :, j * lanes : (j + 1) * lanes]
        return pltpu.make_async_copy(held_ref.at[j], target, sems.at[j])

    for j in range(parts):
        cut = slice(j * lanes, (j + 1) * lanes)
        total = lax.dot_general(
            combined_ref[:, width:], other_ref[cut, :], NT, preferred_element_type=f32
        )
        if j == 0:
            copy.wait()
        total += lax.dot_general(
            combined_ref[:, :width], own_ref[cut, :], NT, preferred_element_type=f32
        )
        held_ref[j] = total.astype(bf16).reshape(peers, rows, lanes)
        send(j).start()
    for j in range(parts):
        send(j).wait()


def back(combined, own_weight, other_weight, peers):
    tokens, chip = combined.shape
    units, width = own_weight.shape
    rows, parts = tokens // peers, 2
    return pl.pallas_call(
        back_kernel,
        in_specs=[INSIDE, OUTSIDE, INSIDE],
        out_specs=pl.BlockSpec(memory_space=pltpu.HBM),
        out_shape=pltpu.HBM((peers, rows, units), bf16),
        scratch_shapes=[
            pltpu.VMEM((units, width), bf16),
            pltpu.VMEM((parts, peers, rows, units // parts), bf16),
            pltpu.SemaphoreType.DMA,
            pltpu.SemaphoreType.DMA((parts,)),
        ],
        compiler_params=kernel_params(),
        cost_estimate=pl.CostEstimate(
            flops=4 * tokens * units * width, bytes_accessed=8 * units * width, transcendentals=0
        ),
        name="back",
    )(*near(combined), far(own_weight), *near(other_weight))


def token_kernel(sums_ref, old_ref, returns_ref, combined_ref, pack_ref, up_ref):
    sums = jnp.sum(sums_ref[...].astype(f32), axis=0)
    square_sum = sums[0:4] + sums[4:8]
    product_sum = sums[8:12] + sums[12:16]
    pack_ref[16:32, :] = sums[16:32]
    old, returns = old_ref[...], returns_ref[...]
    rinv = lax.rsqrt(square_sum / D + EPSILON)
    values = rinv * product_sum
    squash = jnp.tanh((values - old) / CLIP_RANGE)
    clipped = old + CLIP_RANGE * squash
    first = (values - returns) ** 2
    second = (clipped - returns) ** 2
    loss = 0.25 * jnp.sum(first + second)
    dvalue = 0.5 * (values - returns) + 0.5 * (clipped - returns) * (1.0 - squash * squash)
    up = dvalue * rinv
    down = up * rinv * values / D
    pack_ref[0:4, :] = up
    pack_ref[4:8, :] = down
    pack_ref[12:16, :] = jnp.full((4, 128), loss, f32)

    up_ref[...] = jnp.zeros_like(up_ref)
    rest = up
    for i in range(3):
        top = rest.astype(bf16).astype(f32)
        rest = rest - top
        for r in range(4):
            up_ref[i : i + 1, r * 128 : (r + 1) * 128] = top[r : r + 1, :]
    head = jnp.dot(up_ref[...].astype(bf16), combined_ref[...], preferred_element_type=f32)
    head = jnp.sum(head, axis=0, keepdims=True)
    for r in range(4):
        pack_ref[8 + r : 9 + r, :] = head[:, r * 128 : (r + 1) * 128]


def token_terms(sums, old, returns, combined):
    return pl.pallas_call(
        token_kernel,
        in_specs=[INSIDE] * 4,
        out_specs=INSIDE,
        out_shape=jax.ShapeDtypeStruct((32, 128), f32),
        scratch_shapes=[pltpu.VMEM((16, combined.shape[0]), f32)],
        compiler_params=kernel_params(),
        cost_estimate=pl.CostEstimate(flops=4 * combined.size, bytes_accessed=2 * combined.size, transcendentals=0),
        name="token_terms",
    )(sums, old, returns, combined)


def hidden_kernel(spot_ref, arrived_ref, pack_ref, grad_ref):
    spot = spot_ref[0]
    peers, rows, units = arrived_ref.shape
    which = lax.broadcasted_iota(jnp.int32, (4, 128), 0) == spot // 4
    lane = lax.broadcasted_iota(jnp.int32, (rows, 128), 1)
    sub = lax.broadcasted_iota(jnp.int32, (rows, 128), 0)
    pick = lane == sub + lax.rem(spot, 4) * rows

    def column(x):
        line = jnp.sum(jnp.where(which, x, 0.0), axis=0, keepdims=True)
        return jnp.sum(jnp.where(pick, line, 0.0), axis=1, keepdims=True)

    own_up, own_down = column(pack_ref[0:4, :]), column(pack_ref[4:8, :])
    for k in range(units // 128):
        cut = slice(k * 128, (k + 1) * 128)
        total = arrived_ref[0, :, cut].astype(f32)
        for p in range(1, peers):
            total += arrived_ref[p, :, cut].astype(f32)
        part = own_up * pack_ref[16 + k : 17 + k, :] - own_down * total
        grad_ref[:, cut] = part.astype(bf16)


def hidden_gradient(spot, arrived, pack):
    peers, rows, units = arrived.shape
    return pl.pallas_call(
        hidden_kernel,
        grid=(1,),
        in_specs=[pl.BlockSpec(memory_space=pltpu.SMEM), pl.BlockSpec(arrived.shape, lambda i: (0, 0, 0)), INSIDE],
        out_specs=INSIDE,
        out_shape=jax.ShapeDtypeStruct((rows, units), bf16),
        compiler_params=kernel_params(),
        cost_estimate=pl.CostEstimate(
            flops=4 * arrived.size, bytes_accessed=2 * arrived.size, transcendentals=0
        ),
        name="hidden_gradient",
    )(spot.reshape(1), arrived, pack)


def weight_kernel(
    own_pack_ref, other_pack_ref, own_ref, other_ref, scale_ref, hidden_ref, other_hidden_ref,
    out_ref, loss_ref, held_ref, rows_ref, result_ref, in_sems, out_sems,
):
    tokens, width = own_ref.shape
    parts, units = result_ref.shape[:2]
    sources = (hidden_ref, other_hidden_ref)

    def fetch(s):
        return pltpu.make_async_copy(sources[s], held_ref.at[s], in_sems.at[s])

    def send(j):
        part = out_ref.at[j * units : (j + 1) * units, :]
        return pltpu.make_async_copy(result_ref.at[j], part, out_sems.at[j])

    for s in range(2):
        fetch(s).start()
    loss_ref[0, 0] = jnp.max(own_pack_ref[12:13, :]) + jnp.max(other_pack_ref[12:13, :])
    packs = jnp.concatenate(
        [own_pack_ref[0:16, :], other_pack_ref[0:16, :], jnp.zeros((96, 128), f32)], axis=0
    )
    columns = jnp.transpose(packs)
    for s, part_ref in enumerate((own_ref, other_ref)):
        for r in range(tokens // 128):
            up = columns[:, 16 * s + r : 16 * s + r + 1]
            down = columns[:, 16 * s + 4 + r : 16 * s + 5 + r]
            part = part_ref[r * 128 : (r + 1) * 128, :].astype(f32)
            line = up * scale_ref[0:1, :] - down * part
            rows_ref[s * tokens + r * 128 : s * tokens + (r + 1) * 128, :] = line.astype(bf16)
    for s in range(2):
        fetch(s).wait()
    for j in range(parts):
        cut = slice(j * units, (j + 1) * units)
        result_ref[j] = lax.dot_general(
            held_ref[0, :, cut], rows_ref[:tokens, :], TN, preferred_element_type=f32
        ) + lax.dot_general(
            held_ref[1, :, cut], rows_ref[tokens:, :], TN, preferred_element_type=f32
        )
        send(j).start()
    for j in range(parts):
        send(j).wait()


def weight_gradient(own_pack, other_pack, own, other, scale, hidden, other_hidden):
    tokens, units = hidden.shape
    width = own.shape[1]
    parts = 2
    return pl.pallas_call(
        weight_kernel,
        in_specs=[INSIDE] * 5 + [OUTSIDE] * 2,
        out_specs=[pl.BlockSpec(memory_space=pltpu.HBM), pl.BlockSpec(memory_space=pltpu.SMEM)],
        out_shape=[pltpu.HBM((units, width), f32), jax.ShapeDtypeStruct((1, 1), f32)],
        scratch_shapes=[
            pltpu.VMEM((2, tokens, units), bf16),
            pltpu.VMEM((2 * tokens, width), bf16),
            pltpu.VMEM((parts, units // parts, width), f32),
            pltpu.SemaphoreType.DMA((2,)),
            pltpu.SemaphoreType.DMA((parts,)),
        ],
        compiler_params=kernel_params(),
        cost_estimate=pl.CostEstimate(
            flops=4 * units * tokens * width, bytes_accessed=8 * units * width, transcendentals=0
        ),
        name="weight_gradient",
    )(own_pack, other_pack, own, other, scale, far(hidden), far(other_hidden))


def neighbours():
    pairs = [(z, z ^ 1) for z in range(16)]
    return pairs + [(16 + z, 16 + (z + (1 if z % 2 else -1)) % 16) for z in range(16)]


def on_device(
    hidden_act,
    down_weight,
    residual,
    head_weight,
    gain,
    behavior,
    frozen,
    old_values,
    judge_ratings,
    lengths,
):
    yh, core = lax.axis_index("yh"), lax.axis_index("core")
    parity = lax.axis_index("zl")
    z = 2 * lax.axis_index("zh") + parity
    spot = lax.axis_index(PLANE)
    rows_each, units = hidden_act.shape
    width = down_weight.shape[1]
    chip = 2 * width
    group = 16 * rows_each
    section_rows = 8 * rows_each

    hidden = lax.all_to_all(spread(hidden_act, 16), PLANE, 0, 0, tiled=True)
    other_weight = hold(lax.ppermute(down_weight, "core", SWAP))

    chip_scale = lax.dynamic_slice_in_dim(gain * head_weight, yh * chip, chip, 0)
    own_scale = lax.dynamic_slice_in_dim(chip_scale, core * width, width, 0)
    other_scale = lax.dynamic_slice_in_dim(chip_scale, (1 - core) * width, width, 0)
    scale = jnp.concatenate([own_scale, other_scale])

    kept = lax.dynamic_slice_in_dim(residual, z % 8 * rows_each, rows_each, 0)
    sent = lax.dynamic_slice_in_dim(kept, (1 - yh) * chip, chip, 1)
    mine = lax.dynamic_slice_in_dim(kept, yh * chip, chip, 1)
    stream = jnp.where(yh == z // 8, mine, lax.ppermute(sent, "yh", SWAP))
    left, right = stream[:, :width], stream[:, width:]
    stream = jnp.concatenate(
        [jnp.where(core == 0, left, right), jnp.where(core == 0, right, left)], axis=1
    )

    scale_rows = jnp.pad(jnp.stack(pieces(scale, 3)), ((0, 13), (0, 0))).astype(bf16)
    scale_back = lax.dot_general(
        scale_rows[:, :width], down_weight, NT, preferred_element_type=f32
    ) + lax.dot_general(scale_rows[:, width:], other_weight, NT, preferred_element_type=f32)
    base = jnp.sum(scale_back, axis=0).reshape(-1, 128)
    base = jnp.pad(base, ((0, 16 - base.shape[0]), (0, 0))).astype(bf16)
    slot = jnp.arange(group, dtype=jnp.int32)
    token = slot + section_rows * (slot // section_rows + core)
    own_old = jnp.concatenate(
        [
            lax.dynamic_slice_in_dim(old_values, core * section_rows, section_rows, 0),
            lax.dynamic_slice_in_dim(old_values, (2 + core) * section_rows, section_rows, 0),
        ]
    )
    returns = own_old + returns_of(behavior, frozen, old_values, judge_ratings, lengths, token)
    returns, own_old = returns.reshape(4, 128), own_old.reshape(4, 128)
    hidden, returns, own_old, other_weight = lax.optimization_barrier(
        (hidden, returns, own_old, other_weight)
    )

    away = forward(hidden, down_weight, other_weight, 1 - parity, bf16)
    met = lax.ppermute(away, ("core", "zh", "zl"), neighbours())
    kept_half = forward(hidden, down_weight, other_weight, parity, f32)
    hidden, kept_half = lax.optimization_barrier((hidden.reshape(group, units), kept_half))
    far_hidden = lax.ppermute(hidden, "core", SWAP)
    pair = (kept_half + met.astype(f32)).astype(bf16)
    parts = lax.all_to_all(pair.reshape(8, rows_each, chip), "zh", 0, 0, tiled=True)
    combined = (jnp.sum(parts.astype(f32), axis=0) + stream.astype(f32)).astype(bf16)
    combined = lax.all_gather(combined, ("zh", "zl"), axis=0, tiled=True)
    own_columns, other_columns = combined[:, :width], combined[:, width:]

    sums = token_sums(combined, scale_rows, base, 16)
    sums = lax.all_to_all(sums, PLANE, 0, 0, tiled=True)
    payload = back(combined, down_weight, other_weight, 16)
    sums, payload = lax.optimization_barrier((sums, payload))
    arrived = lax.all_to_all(payload, PLANE, 0, 0, tiled=True)
    far_columns = lax.ppermute(other_columns, "core", SWAP)
    pack = token_terms(sums, own_old, returns, combined)
    hidden_grad = hidden_gradient(spot, arrived, pack)
    other_pack = lax.ppermute(pack, "core", SWAP)
    weight_grad, total_loss = weight_gradient(
        pack, other_pack, own_columns, far_columns, own_scale.reshape(1, -1), hidden, far_hidden
    )
    own_head = pack[8:10] + other_pack[10:12]
    other_head = pack[10:12] + other_pack[8:10]
    head_chip = jnp.concatenate(
        [jnp.where(core == 0, own_head, other_head), jnp.where(core == 0, other_head, own_head)]
    )
    head_far = lax.ppermute(head_chip, "yh", SWAP)
    head_far, total_loss = lax.optimization_barrier((head_far, total_loss))
    head_sum = jnp.concatenate(
        [jnp.where(yh == 0, head_chip, head_far), jnp.where(yh == 0, head_far, head_chip)]
    )
    head_grad = gain * head_sum.reshape(-1)
    return (total_loss[0, 0], head_grad, weight_grad, hidden_grad)


def solution(mesh):
    axes = ("yh", "core", "x", "yl", "zh", "zl")
    fine = Mesh(mesh.devices.reshape(2, 2, 4, 2, 8, 2), axes)
    tp = ("zh", "zl")
    in_specs = (
        P(("yh", "core", "x", "yl"), tp),
        P(tp, ("x", "yl", "yh", "core")),
        P(("yh", "core"), ("x", "yl")),
        P(("x", "yl")),
        P(("x", "yl")),
        P(),
        P(),
        P(),
        P(),
        P(),
    )
    out_specs = (
        P(),
        P(("x", "yl")),
        P(tp, ("x", "yl", "yh", "core")),
        P(("yh", "core", "x", "yl"), tp),
    )
    return jax.shard_map(
        on_device, mesh=fine, in_specs=in_specs, out_specs=out_specs, check_vma=False
    )
```

```python
import jax
import jax.numpy as jnp
from jax import lax
from jax.experimental import pallas as pl
from jax.experimental.pallas import tpu as pltpu
from jax.sharding import Mesh, PartitionSpec as P

D = 8192
KL_PENALTY_SCALE = 0.1
TRACE_DECAY = 0.95
CLIP_RANGE = 0.2
EPSILON = 1e-05

PLANE = ("yh", "x", "yl")
SWAP = [(0, 1), (1, 0)]
f32, bf16 = jnp.float32, jnp.bfloat16


def returns_of(behavior, frozen, old_values, judge_ratings, lengths, rows):
    total = behavior.shape[0]
    position = jnp.arange(total, dtype=jnp.int32)
    ends = jnp.cumsum(lengths)
    closes = position[:, None] == ends[None, :] - 1
    final = jnp.any(closes, axis=1)
    extra = jnp.sum(jnp.where(closes, judge_ratings[None, :], 0.0), axis=1)
    rewards = extra - KL_PENALTY_SCALE * (behavior - frozen)
    following = jnp.concatenate([old_values[1:], jnp.zeros_like(old_values[:1])])
    delta = rewards + jnp.where(final, 0.0, following) - old_values
    segment = jnp.sum((position[:, None] >= ends[None, :]).astype(jnp.int32), axis=1)
    row_seg = jnp.sum((rows[:, None] >= ends[None, :]).astype(jnp.int32), axis=1)
    gap = position[None, :] - rows[:, None]
    inside = (row_seg[:, None] == segment[None, :]) & (gap >= 0)
    powers = jnp.power(jnp.float32(TRACE_DECAY), jnp.maximum(gap, 0).astype(f32))
    return jnp.sum(jnp.where(inside, powers, 0.0) * delta[None, :], axis=1)


def pieces(x, count):
    out = []
    for _ in range(count):
        top = lax.reduce_precision(x, 8, 7)
        out.append(top)
        x = x - top
    return out


def kernel_params():
    return pltpu.CompilerParams(vmem_limit_bytes=16 * 1024 * 1024)


NT = (((1,), (1,)), ((), ()))
TN = (((0,), (0,)), ((), ()))
INSIDE = pl.BlockSpec(memory_space=pltpu.VMEM)
OUTSIDE = pl.BlockSpec(memory_space=pl.ANY)


def near(*arrays):
    return [pltpu.with_memory_space_constraint(a, pltpu.VMEM) for a in arrays]


def far(array):
    return pltpu.with_memory_space_constraint(array, pltpu.HBM)


def hold_kernel(in_ref, out_ref, sem):
    copy = pltpu.make_async_copy(in_ref, out_ref, sem)
    copy.start()
    copy.wait()


def hold(x):
    return pl.pallas_call(
        hold_kernel,
        in_specs=[pl.BlockSpec(memory_space=pl.ANY)],
        out_specs=INSIDE,
        out_shape=pltpu.VMEM(x.shape, x.dtype),
        scratch_shapes=[pltpu.SemaphoreType.DMA],
        compiler_params=kernel_params(),
        cost_estimate=pl.CostEstimate(flops=0, bytes_accessed=4 * x.size, transcendentals=0),
        name="hold",
    )(x)


def spread_kernel(in_ref, out_ref, held_ref, sem, sems):
    first = pltpu.make_async_copy(in_ref, held_ref, sem)
    first.start()
    first.wait()
    copies = [
        pltpu.make_async_copy(held_ref, out_ref.at[i], sems.at[i]) for i in range(out_ref.shape[0])
    ]
    for copy in copies:
        copy.start()
    for copy in copies:
        copy.wait()


def spread(x, count):
    return pl.pallas_call(
        spread_kernel,
        in_specs=[pl.BlockSpec(memory_space=pl.ANY)],
        out_specs=pl.BlockSpec(memory_space=pltpu.HBM),
        out_shape=pltpu.HBM((count,) + x.shape, x.dtype),
        scratch_shapes=[
            pltpu.VMEM(x.shape, x.dtype),
            pltpu.SemaphoreType.DMA,
            pltpu.SemaphoreType.DMA((count,)),
        ],
        compiler_params=kernel_params(),
        cost_estimate=pl.CostEstimate(flops=0, bytes_accessed=2 * count * x.size, transcendentals=0),
        name="spread",
    )(x)


def forward_kernel(half_ref, hidden_ref, own_ref, other_ref, out_ref):
    half = hidden_ref[:, pl.ds(half_ref[0], 1)]
    rows = half.reshape(out_ref.shape[0], hidden_ref.shape[-1])
    width = own_ref.shape[1]
    for i, w_ref in enumerate((own_ref, other_ref)):
        product = jnp.dot(rows, w_ref[...], preferred_element_type=f32)
        out_ref[:, i * width : (i + 1) * width] = product.astype(out_ref.dtype)


def forward(hidden, own_weight, other_weight, half, dtype):
    count, rows, units = hidden.shape
    width = own_weight.shape[1]
    tokens = count // 2 * rows
    return pl.pallas_call(
        forward_kernel,
        in_specs=[pl.BlockSpec(memory_space=pltpu.SMEM)] + [INSIDE] * 3,
        out_specs=INSIDE,
        out_shape=jax.ShapeDtypeStruct((tokens, 2 * width), dtype),
        compiler_params=kernel_params(),
        cost_estimate=pl.CostEstimate(
            flops=4 * tokens * units * width, bytes_accessed=4 * units * width, transcendentals=0
        ),
        name="forward",
    )(half.reshape(1), *near(hidden.reshape(count // 2, 2, rows, units), own_weight, other_weight))


def sums_kernel(combined_ref, scale_ref, base_ref, out_ref, held_ref, rows_ref, sem):
    peers, rows, lanes = out_ref.shape
    both = combined_ref[...]
    wide = both.astype(f32)
    square = wide * wide
    top = square.astype(bf16)
    rest = (square - top.astype(f32)).astype(bf16)
    ones = jnp.ones((16, both.shape[1]), bf16)
    squares = lax.dot_general(ones, top, NT, preferred_element_type=f32)
    squares += lax.dot_general(ones, rest, NT, preferred_element_type=f32)
    products = lax.dot_general(scale_ref[...], both, NT, preferred_element_type=f32)
    place = 0
    for line in (squares[0:1], jnp.sum(products, axis=0, keepdims=True)):
        top = line.astype(bf16).astype(f32)
        for part in (top, line - top):
            for i in range(4):
                rows_ref[place : place + 1, :] = part[:, i * lanes : (i + 1) * lanes]
                place += 1
    sums = rows_ref[...].astype(bf16)
    held_ref[:, :16, :] = jnp.broadcast_to(sums[None], (peers, 16, lanes))
    held_ref[:, 16:, :] = jnp.broadcast_to(base_ref[...][None], (peers, rows - 16, lanes))
    copy = pltpu.make_async_copy(held_ref, out_ref, sem)
    copy.start()
    copy.wait()


def token_sums(combined, scale_rows, base, peers):
    shape = (peers, 32, 128)
    return pl.pallas_call(
        sums_kernel,
        in_specs=[INSIDE] * 3,
        out_specs=pl.BlockSpec(memory_space=pltpu.HBM),
        out_shape=pltpu.HBM(shape, bf16),
        scratch_shapes=[pltpu.VMEM(shape, bf16), pltpu.VMEM((16, 128), f32), pltpu.SemaphoreType.DMA],
        compiler_params=kernel_params(),
        cost_estimate=pl.CostEstimate(flops=96 * combined.size, bytes_accessed=2 * combined.size, transcendentals=0),
        name="token_sums",
    )(*near(combined), scale_rows, base)


def back_kernel(combined_ref, outer_ref, other_ref, out_ref, own_ref, held_ref, sem, sems):
    copy = pltpu.make_async_copy(outer_ref, own_ref, sem)
    copy.start()
    width = own_ref.shape[1]
    parts, peers, rows, lanes = held_ref.shape

    def send(j):
        target = out_ref.at[:, :, j * lanes : (j + 1) * lanes]
        return pltpu.make_async_copy(held_ref.at[j], target, sems.at[j])

    for j in range(parts):
        cut = slice(j * lanes, (j + 1) * lanes)
        total = lax.dot_general(
            combined_ref[:, width:], other_ref[cut, :], NT, preferred_element_type=f32
        )
        if j == 0:
            copy.wait()
        total += lax.dot_general(
            combined_ref[:, :width], own_ref[cut, :], NT, preferred_element_type=f32
        )
        held_ref[j] = total.astype(bf16).reshape(peers, rows, lanes)
        send(j).start()
    for j in range(parts):
        send(j).wait()


def back(combined, own_weight, other_weight, peers):
    tokens, chip = combined.shape
    units, width = own_weight.shape
    rows, parts = tokens // peers, 2
    return pl.pallas_call(
        back_kernel,
        in_specs=[INSIDE, OUTSIDE, INSIDE],
        out_specs=pl.BlockSpec(memory_space=pltpu.HBM),
        out_shape=pltpu.HBM((peers, rows, units), bf16),
        scratch_shapes=[
            pltpu.VMEM((units, width), bf16),
            pltpu.VMEM((parts, peers, rows, units // parts), bf16),
            pltpu.SemaphoreType.DMA,
            pltpu.SemaphoreType.DMA((parts,)),
        ],
        compiler_params=kernel_params(),
        cost_estimate=pl.CostEstimate(
            flops=4 * tokens * units * width, bytes_accessed=8 * units * width, transcendentals=0
        ),
        name="back",
    )(*near(combined), far(own_weight), *near(other_weight))


def token_kernel(sums_ref, old_ref, returns_ref, combined_ref, pack_ref, up_ref):
    sums = jnp.sum(sums_ref[...].astype(f32), axis=0)
    square_sum = sums[0:4] + sums[4:8]
    product_sum = sums[8:12] + sums[12:16]
    pack_ref[16:32, :] = sums[16:32]
    old, returns = old_ref[...], returns_ref[...]
    rinv = lax.rsqrt(square_sum / D + EPSILON)
    values = rinv * product_sum
    squash = jnp.tanh((values - old) / CLIP_RANGE)
    clipped = old + CLIP_RANGE * squash
    first = (values - returns) ** 2
    second = (clipped - returns) ** 2
    loss = 0.25 * jnp.sum(first + second)
    dvalue = 0.5 * (values - returns) + 0.5 * (clipped - returns) * (1.0 - squash * squash)
    up = dvalue * rinv
    down = up * rinv * values / D
    pack_ref[0:4, :] = up
    pack_ref[4:8, :] = down
    pack_ref[12:16, :] = jnp.full((4, 128), loss, f32)

    up_ref[...] = jnp.zeros_like(up_ref)
    rest = up
    for i in range(3):
        top = rest.astype(bf16).astype(f32)
        rest = rest - top
        for r in range(4):
            up_ref[i : i + 1, r * 128 : (r + 1) * 128] = top[r : r + 1, :]
    head = jnp.dot(up_ref[...].astype(bf16), combined_ref[...], preferred_element_type=f32)
    head = jnp.sum(head, axis=0, keepdims=True)
    for r in range(4):
        pack_ref[8 + r : 9 + r, :] = head[:, r * 128 : (r + 1) * 128]


def token_terms(sums, old, returns, combined):
    return pl.pallas_call(
        token_kernel,
        in_specs=[INSIDE] * 4,
        out_specs=INSIDE,
        out_shape=jax.ShapeDtypeStruct((32, 128), f32),
        scratch_shapes=[pltpu.VMEM((16, combined.shape[0]), f32)],
        compiler_params=kernel_params(),
        cost_estimate=pl.CostEstimate(flops=4 * combined.size, bytes_accessed=2 * combined.size, transcendentals=0),
        name="token_terms",
    )(sums, old, returns, combined)


def hidden_kernel(spot_ref, arrived_ref, pack_ref, grad_ref):
    spot = spot_ref[0]
    peers, rows, units = arrived_ref.shape
    which = lax.broadcasted_iota(jnp.int32, (4, 128), 0) == spot // 4
    lane = lax.broadcasted_iota(jnp.int32, (rows, 128), 1)
    sub = lax.broadcasted_iota(jnp.int32, (rows, 128), 0)
    pick = lane == sub + lax.rem(spot, 4) * rows

    def column(x):
        line = jnp.sum(jnp.where(which, x, 0.0), axis=0, keepdims=True)
        return jnp.sum(jnp.where(pick, line, 0.0), axis=1, keepdims=True)

    own_up, own_down = column(pack_ref[0:4, :]), column(pack_ref[4:8, :])
    for k in range(units // 128):
        cut = slice(k * 128, (k + 1) * 128)
        total = arrived_ref[0, :, cut].astype(f32)
        for p in range(1, peers):
            total += arrived_ref[p, :, cut].astype(f32)
        part = own_up * pack_ref[16 + k : 17 + k, :] - own_down * total
        grad_ref[:, cut] = part.astype(bf16)


def hidden_gradient(spot, arrived, pack):
    peers, rows, units = arrived.shape
    return pl.pallas_call(
        hidden_kernel,
        grid=(1,),
        in_specs=[pl.BlockSpec(memory_space=pltpu.SMEM), pl.BlockSpec(arrived.shape, lambda i: (0, 0, 0)), INSIDE],
        out_specs=INSIDE,
        out_shape=jax.ShapeDtypeStruct((rows, units), bf16),
        compiler_params=kernel_params(),
        cost_estimate=pl.CostEstimate(
            flops=4 * arrived.size, bytes_accessed=2 * arrived.size, transcendentals=0
        ),
        name="hidden_gradient",
    )(spot.reshape(1), arrived, pack)


def weight_kernel(
    own_pack_ref, other_pack_ref, own_ref, other_ref, scale_ref, hidden_ref, other_hidden_ref,
    out_ref, loss_ref, held_ref, rows_ref, result_ref, in_sems, out_sems,
):
    tokens, width = own_ref.shape
    parts, units = result_ref.shape[:2]
    sources = (hidden_ref, other_hidden_ref)

    def fetch(s):
        return pltpu.make_async_copy(sources[s], held_ref.at[s], in_sems.at[s])

    def send(j):
        part = out_ref.at[j * units : (j + 1) * units, :]
        return pltpu.make_async_copy(result_ref.at[j], part, out_sems.at[j])

    for s in range(2):
        fetch(s).start()
    loss_ref[0, 0] = jnp.max(own_pack_ref[12:13, :]) + jnp.max(other_pack_ref[12:13, :])
    packs = jnp.concatenate(
        [own_pack_ref[0:16, :], other_pack_ref[0:16, :], jnp.zeros((96, 128), f32)], axis=0
    )
    columns = jnp.transpose(packs)
    for s, part_ref in enumerate((own_ref, other_ref)):
        for r in range(tokens // 128):
            up = columns[:, 16 * s + r : 16 * s + r + 1]
            down = columns[:, 16 * s + 4 + r : 16 * s + 5 + r]
            part = part_ref[r * 128 : (r + 1) * 128, :].astype(f32)
            line = up * scale_ref[0:1, :] - down * part
            rows_ref[s * tokens + r * 128 : s * tokens + (r + 1) * 128, :] = line.astype(bf16)
    for s in range(2):
        fetch(s).wait()
    for j in range(parts):
        cut = slice(j * units, (j + 1) * units)
        result_ref[j] = lax.dot_general(
            held_ref[0, :, cut], rows_ref[:tokens, :], TN, preferred_element_type=f32
        ) + lax.dot_general(
            held_ref[1, :, cut], rows_ref[tokens:, :], TN, preferred_element_type=f32
        )
        send(j).start()
    for j in range(parts):
        send(j).wait()


def weight_gradient(own_pack, other_pack, own, other, scale, hidden, other_hidden):
    tokens, units = hidden.shape
    width = own.shape[1]
    parts = 2
    return pl.pallas_call(
        weight_kernel,
        in_specs=[INSIDE] * 5 + [OUTSIDE] * 2,
        out_specs=[pl.BlockSpec(memory_space=pltpu.HBM), pl.BlockSpec(memory_space=pltpu.SMEM)],
        out_shape=[pltpu.HBM((units, width), f32), jax.ShapeDtypeStruct((1, 1), f32)],
        scratch_shapes=[
            pltpu.VMEM((2, tokens, units), bf16),
            pltpu.VMEM((2 * tokens, width), bf16),
            pltpu.VMEM((parts, units // parts, width), f32),
            pltpu.SemaphoreType.DMA((2,)),
            pltpu.SemaphoreType.DMA((parts,)),
        ],
        compiler_params=kernel_params(),
        cost_estimate=pl.CostEstimate(
            flops=4 * units * tokens * width, bytes_accessed=8 * units * width, transcendentals=0
        ),
        name="weight_gradient",
    )(own_pack, other_pack, own, other, scale, hidden, other_hidden)


def neighbours():
    pairs = [(z, z ^ 1) for z in range(16)]
    return pairs + [(16 + z, 16 + (z + (1 if z % 2 else -1)) % 16) for z in range(16)]


def on_device(
    hidden_act,
    down_weight,
    residual,
    head_weight,
    gain,
    behavior,
    frozen,
    old_values,
    judge_ratings,
    lengths,
):
    yh, core = lax.axis_index("yh"), lax.axis_index("core")
    parity = lax.axis_index("zl")
    z = 2 * lax.axis_index("zh") + parity
    spot = lax.axis_index(PLANE)
    rows_each, units = hidden_act.shape
    width = down_weight.shape[1]
    chip = 2 * width
    group = 16 * rows_each
    section_rows = 8 * rows_each

    hidden = lax.all_to_all(spread(hidden_act, 16), PLANE, 0, 0, tiled=True)
    other_weight = hold(lax.ppermute(down_weight, "core", SWAP))

    chip_scale = lax.dynamic_slice_in_dim(gain * head_weight, yh * chip, chip, 0)
    own_scale = lax.dynamic_slice_in_dim(chip_scale, core * width, width, 0)
    other_scale = lax.dynamic_slice_in_dim(chip_scale, (1 - core) * width, width, 0)
    scale = jnp.concatenate([own_scale, other_scale])

    kept = lax.dynamic_slice_in_dim(residual, z % 8 * rows_each, rows_each, 0)
    sent = lax.dynamic_slice_in_dim(kept, (1 - yh) * chip, chip, 1)
    mine = lax.dynamic_slice_in_dim(kept, yh * chip, chip, 1)
    stream = jnp.where(yh == z // 8, mine, lax.ppermute(sent, "yh", SWAP))
    left, right = stream[:, :width], stream[:, width:]
    stream = jnp.concatenate(
        [jnp.where(core == 0, left, right), jnp.where(core == 0, right, left)], axis=1
    )

    scale_rows = jnp.pad(jnp.stack(pieces(scale, 3)), ((0, 13), (0, 0))).astype(bf16)
    scale_back = lax.dot_general(
        scale_rows[:, :width], down_weight, NT, preferred_element_type=f32
    ) + lax.dot_general(scale_rows[:, width:], other_weight, NT, preferred_element_type=f32)
    base = jnp.sum(scale_back, axis=0).reshape(-1, 128)
    base = jnp.pad(base, ((0, 16 - base.shape[0]), (0, 0))).astype(bf16)
    slot = jnp.arange(group, dtype=jnp.int32)
    token = slot + section_rows * (slot // section_rows + core)
    own_old = jnp.concatenate(
        [
            lax.dynamic_slice_in_dim(old_values, core * section_rows, section_rows, 0),
            lax.dynamic_slice_in_dim(old_values, (2 + core) * section_rows, section_rows, 0),
        ]
    )
    returns = own_old + returns_of(behavior, frozen, old_values, judge_ratings, lengths, token)
    returns, own_old = returns.reshape(4, 128), own_old.reshape(4, 128)
    hidden, returns, own_old, other_weight = lax.optimization_barrier(
        (hidden, returns, own_old, other_weight)
    )

    away = forward(hidden, down_weight, other_weight, 1 - parity, bf16)
    met = lax.ppermute(away, ("core", "zh", "zl"), neighbours())
    kept_half = forward(hidden, down_weight, other_weight, parity, f32)
    hidden, kept_half = lax.optimization_barrier((hidden.reshape(group, units), kept_half))
    far_hidden = lax.ppermute(hidden, "core", SWAP)
    pair = (kept_half + met.astype(f32)).astype(bf16)
    parts = lax.all_to_all(pair.reshape(8, rows_each, chip), "zh", 0, 0, tiled=True)
    combined = (jnp.sum(parts.astype(f32), axis=0) + stream.astype(f32)).astype(bf16)
    combined = lax.all_gather(combined, ("zh", "zl"), axis=0, tiled=True)
    own_columns, other_columns = combined[:, :width], combined[:, width:]

    sums = token_sums(combined, scale_rows, base, 16)
    sums = lax.all_to_all(sums, PLANE, 0, 0, tiled=True)
    payload = back(combined, down_weight, other_weight, 16)
    sums, payload = lax.optimization_barrier((sums, payload))
    arrived = lax.all_to_all(payload, PLANE, 0, 0, tiled=True)
    far_columns = lax.ppermute(other_columns, "core", SWAP)
    pack = token_terms(sums, own_old, returns, combined)
    hidden_grad = hidden_gradient(spot, arrived, pack)
    other_pack = lax.ppermute(pack, "core", SWAP)
    weight_grad, total_loss = weight_gradient(
        pack, other_pack, own_columns, far_columns, own_scale.reshape(1, -1), hidden, far_hidden
    )
    own_head = pack[8:10] + other_pack[10:12]
    other_head = pack[10:12] + other_pack[8:10]
    head_chip = jnp.concatenate(
        [jnp.where(core == 0, own_head, other_head), jnp.where(core == 0, other_head, own_head)]
    )
    head_far = lax.ppermute(head_chip, "yh", SWAP)
    head_far, total_loss = lax.optimization_barrier((head_far, total_loss))
    head_sum = jnp.concatenate(
        [jnp.where(yh == 0, head_chip, head_far), jnp.where(yh == 0, head_far, head_chip)]
    )
    head_grad = gain * head_sum.reshape(-1)
    return (total_loss[0, 0], head_grad, weight_grad, hidden_grad)


def solution(mesh):
    axes = ("yh", "core", "x", "yl", "zh", "zl")
    fine = Mesh(mesh.devices.reshape(2, 2, 4, 2, 8, 2), axes)
    tp = ("zh", "zl")
    in_specs = (
        P(("yh", "core", "x", "yl"), tp),
        P(tp, ("x", "yl", "yh", "core")),
        P(("yh", "core"), ("x", "yl")),
        P(("x", "yl")),
        P(("x", "yl")),
        P(),
        P(),
        P(),
        P(),
        P(),
    )
    out_specs = (
        P(),
        P(("x", "yl")),
        P(tp, ("x", "yl", "yh", "core")),
        P(("yh", "core", "x", "yl"), tp),
    )
    return jax.shard_map(
        on_device, mesh=fine, in_specs=in_specs, out_specs=out_specs, check_vma=False
    )
```

```python
import jax
import jax.numpy as jnp
from jax import lax
from jax.experimental import pallas as pl
from jax.experimental.pallas import tpu as pltpu
from jax.sharding import Mesh, PartitionSpec as P

D = 8192
KL_PENALTY_SCALE = 0.1
TRACE_DECAY = 0.95
CLIP_RANGE = 0.2
EPSILON = 1e-05

SECTION = ("yh", "core", "x", "yl")
SWAP = [(0, 1), (1, 0)]
f32, bf16 = jnp.float32, jnp.bfloat16


def returns_of(behavior, frozen, old_values, judge_ratings, lengths, rows):
    total = behavior.shape[0]
    position = jnp.arange(total, dtype=jnp.int32)
    ends = jnp.cumsum(lengths)
    closes = position[:, None] == ends[None, :] - 1
    final = jnp.any(closes, axis=1)
    extra = jnp.sum(jnp.where(closes, judge_ratings[None, :], 0.0), axis=1)
    rewards = extra - KL_PENALTY_SCALE * (behavior - frozen)
    following = jnp.concatenate([old_values[1:], jnp.zeros_like(old_values[:1])])
    delta = rewards + jnp.where(final, 0.0, following) - old_values
    segment = jnp.sum((position[:, None] >= ends[None, :]).astype(jnp.int32), axis=1)
    row_seg = jnp.sum((rows[:, None] >= ends[None, :]).astype(jnp.int32), axis=1)
    gap = position[None, :] - rows[:, None]
    inside = (row_seg[:, None] == segment[None, :]) & (gap >= 0)
    powers = jnp.power(jnp.float32(TRACE_DECAY), jnp.maximum(gap, 0).astype(f32))
    here = jnp.sum(jnp.where(gap == 0, old_values[None, :], 0.0), axis=1)
    return here, jnp.sum(jnp.where(inside, powers, 0.0) * delta[None, :], axis=1)


def pieces(x, count):
    out = []
    for _ in range(count):
        top = lax.reduce_precision(x, 8, 7)
        out.append(top)
        x = x - top
    return out


def kernel_params():
    return pltpu.CompilerParams(vmem_limit_bytes=16 * 1024 * 1024)


NT = (((1,), (1,)), ((), ()))
TN = (((0,), (0,)), ((), ()))
INSIDE = pl.BlockSpec(memory_space=pltpu.VMEM)
OUTSIDE = pl.BlockSpec(memory_space=pl.ANY)


def near(*arrays):
    return [pltpu.with_memory_space_constraint(a, pltpu.VMEM) for a in arrays]


def far(array):
    return pltpu.with_memory_space_constraint(array, pltpu.HBM)


def hold_kernel(in_ref, out_ref, sem):
    copy = pltpu.make_async_copy(in_ref, out_ref, sem)
    copy.start()
    copy.wait()


def hold(x):
    return pl.pallas_call(
        hold_kernel,
        in_specs=[pl.BlockSpec(memory_space=pl.ANY)],
        out_specs=INSIDE,
        out_shape=pltpu.VMEM(x.shape, x.dtype),
        scratch_shapes=[pltpu.SemaphoreType.DMA],
        compiler_params=kernel_params(),
        cost_estimate=pl.CostEstimate(flops=0, bytes_accessed=4 * x.size, transcendentals=0),
        name="hold",
    )(x)


def spread_kernel(in_ref, out_ref, held_ref, sem, sems):
    first = pltpu.make_async_copy(in_ref, held_ref, sem)
    first.start()
    first.wait()
    copies = [
        pltpu.make_async_copy(held_ref, out_ref.at[i], sems.at[i]) for i in range(out_ref.shape[0])
    ]
    for copy in copies:
        copy.start()
    for copy in copies:
        copy.wait()


def spread(x, count):
    return pl.pallas_call(
        spread_kernel,
        in_specs=[pl.BlockSpec(memory_space=pl.ANY)],
        out_specs=pl.BlockSpec(memory_space=pltpu.HBM),
        out_shape=pltpu.HBM((count,) + x.shape, x.dtype),
        scratch_shapes=[
            pltpu.VMEM(x.shape, x.dtype),
            pltpu.SemaphoreType.DMA,
            pltpu.SemaphoreType.DMA((count,)),
        ],
        compiler_params=kernel_params(),
        cost_estimate=pl.CostEstimate(flops=0, bytes_accessed=2 * count * x.size, transcendentals=0),
        name="spread",
    )(x)


def forward_kernel(half_ref, hidden_ref, own_ref, other_ref, out_ref):
    half = hidden_ref[:, pl.ds(half_ref[0], 1)]
    rows = half.reshape(out_ref.shape[0], hidden_ref.shape[-1])
    width = own_ref.shape[1]
    for i, w_ref in enumerate((own_ref, other_ref)):
        product = jnp.dot(rows, w_ref[...], preferred_element_type=f32)
        out_ref[:, i * width : (i + 1) * width] = product.astype(out_ref.dtype)


def forward(hidden, own_weight, other_weight, half, dtype):
    count, rows, units = hidden.shape
    width = own_weight.shape[1]
    tokens = count // 2 * rows
    return pl.pallas_call(
        forward_kernel,
        in_specs=[pl.BlockSpec(memory_space=pltpu.SMEM)] + [INSIDE] * 3,
        out_specs=INSIDE,
        out_shape=jax.ShapeDtypeStruct((tokens, 2 * width), dtype),
        compiler_params=kernel_params(),
        cost_estimate=pl.CostEstimate(
            flops=4 * tokens * units * width, bytes_accessed=4 * units * width, transcendentals=0
        ),
        name="forward",
    )(half.reshape(1), *near(hidden.reshape(count // 2, 2, rows, units), own_weight, other_weight))


def sums_kernel(combined_ref, scale_ref, base_ref, out_ref, held_ref, rows_ref, sem):
    peers, rows, lanes = out_ref.shape
    both = combined_ref[...]
    wide = both.astype(f32)
    square = wide * wide
    top = square.astype(bf16)
    rest = (square - top.astype(f32)).astype(bf16)
    ones = jnp.ones((16, both.shape[1]), bf16)
    squares = lax.dot_general(ones, top, NT, preferred_element_type=f32)
    squares += lax.dot_general(ones, rest, NT, preferred_element_type=f32)
    products = lax.dot_general(scale_ref[...], both, NT, preferred_element_type=f32)
    place = 0
    for line in (squares[0:1], jnp.sum(products, axis=0, keepdims=True)):
        top = line.astype(bf16).astype(f32)
        for part in (top, line - top):
            for i in range(4):
                rows_ref[place : place + 1, :] = part[:, i * lanes : (i + 1) * lanes]
                place += 1
    sums = rows_ref[...].astype(bf16)
    held_ref[:, :16, :] = jnp.broadcast_to(sums[None], (peers, 16, lanes))
    held_ref[:, 16:, :] = jnp.broadcast_to(base_ref[...][None], (peers, rows - 16, lanes))
    copy = pltpu.make_async_copy(held_ref, out_ref, sem)
    copy.start()
    copy.wait()


def token_sums(combined, scale_rows, base, peers):
    shape = (peers, 32, 128)
    return pl.pallas_call(
        sums_kernel,
        in_specs=[INSIDE] * 3,
        out_specs=pl.BlockSpec(memory_space=pltpu.HBM),
        out_shape=pltpu.HBM(shape, bf16),
        scratch_shapes=[pltpu.VMEM(shape, bf16), pltpu.VMEM((16, 128), f32), pltpu.SemaphoreType.DMA],
        compiler_params=kernel_params(),
        cost_estimate=pl.CostEstimate(flops=96 * combined.size, bytes_accessed=2 * combined.size, transcendentals=0),
        name="token_sums",
    )(*near(combined), scale_rows, base)


def back_kernel(combined_ref, outer_ref, other_ref, out_ref, own_ref, held_ref, sem, sems):
    copy = pltpu.make_async_copy(outer_ref, own_ref, sem)
    copy.start()
    width = own_ref.shape[1]
    parts, peers, rows, lanes = held_ref.shape

    def send(j):
        target = out_ref.at[:, :, j * lanes : (j + 1) * lanes]
        return pltpu.make_async_copy(held_ref.at[j], target, sems.at[j])

    for j in range(parts):
        cut = slice(j * lanes, (j + 1) * lanes)
        total = lax.dot_general(
            combined_ref[:, width:], other_ref[cut, :], NT, preferred_element_type=f32
        )
        if j == 0:
            copy.wait()
        total += lax.dot_general(
            combined_ref[:, :width], own_ref[cut, :], NT, preferred_element_type=f32
        )
        held_ref[j] = total.astype(bf16).reshape(peers, rows, lanes)
        send(j).start()
    for j in range(parts):
        send(j).wait()


def back(combined, own_weight, other_weight, peers):
    tokens, chip = combined.shape
    units, width = own_weight.shape
    rows, parts = tokens // peers, 2
    return pl.pallas_call(
        back_kernel,
        in_specs=[INSIDE, OUTSIDE, INSIDE],
        out_specs=pl.BlockSpec(memory_space=pltpu.HBM),
        out_shape=pltpu.HBM((peers, rows, units), bf16),
        scratch_shapes=[
            pltpu.VMEM((units, width), bf16),
            pltpu.VMEM((parts, peers, rows, units // parts), bf16),
            pltpu.SemaphoreType.DMA,
            pltpu.SemaphoreType.DMA((parts,)),
        ],
        compiler_params=kernel_params(),
        cost_estimate=pl.CostEstimate(
            flops=4 * tokens * units * width, bytes_accessed=8 * units * width, transcendentals=0
        ),
        name="back",
    )(*near(combined), far(own_weight), *near(other_weight))


def token_kernel(sums_ref, old_ref, returns_ref, combined_ref, pack_ref, up_ref):
    sums = jnp.sum(sums_ref[...].astype(f32), axis=0)
    square_sum = sums[0:4] + sums[4:8]
    product_sum = sums[8:12] + sums[12:16]
    pack_ref[16:32, :] = sums[16:32]
    old, returns = old_ref[...], returns_ref[...]
    rinv = lax.rsqrt(square_sum / D + EPSILON)
    values = rinv * product_sum
    squash = jnp.tanh((values - old) / CLIP_RANGE)
    clipped = old + CLIP_RANGE * squash
    first = (values - returns) ** 2
    second = (clipped - returns) ** 2
    loss = 0.25 * jnp.sum(first + second)
    dvalue = 0.5 * (values - returns) + 0.5 * (clipped - returns) * (1.0 - squash * squash)
    up = dvalue * rinv
    down = up * rinv * values / D
    pack_ref[0:4, :] = up
    pack_ref[4:8, :] = down
    pack_ref[12:16, :] = jnp.full((4, 128), loss, f32)

    up_ref[...] = jnp.zeros_like(up_ref)
    rest = up
    for i in range(3):
        top = rest.astype(bf16).astype(f32)
        rest = rest - top
        for r in range(4):
            up_ref[i : i + 1, r * 128 : (r + 1) * 128] = top[r : r + 1, :]
    head = jnp.dot(up_ref[...].astype(bf16), combined_ref[...], preferred_element_type=f32)
    head = jnp.sum(head, axis=0, keepdims=True)
    for r in range(4):
        pack_ref[8 + r : 9 + r, :] = head[:, r * 128 : (r + 1) * 128]


def token_terms(sums, old, returns, combined):
    return pl.pallas_call(
        token_kernel,
        in_specs=[INSIDE] * 4,
        out_specs=INSIDE,
        out_shape=jax.ShapeDtypeStruct((32, 128), f32),
        scratch_shapes=[pltpu.VMEM((16, combined.shape[0]), f32)],
        compiler_params=kernel_params(),
        cost_estimate=pl.CostEstimate(flops=4 * combined.size, bytes_accessed=2 * combined.size, transcendentals=0),
        name="token_terms",
    )(sums, old, returns, combined)


def hidden_kernel(spot_ref, arrived_ref, pack_ref, grad_ref):
    spot = spot_ref[0]
    peers, rows, units = arrived_ref.shape
    which = lax.broadcasted_iota(jnp.int32, (4, 128), 0) == spot // 4
    lane = lax.broadcasted_iota(jnp.int32, (rows, 128), 1)
    sub = lax.broadcasted_iota(jnp.int32, (rows, 128), 0)
    pick = lane == sub + lax.rem(spot, 4) * rows

    def column(x):
        line = jnp.sum(jnp.where(which, x, 0.0), axis=0, keepdims=True)
        return jnp.sum(jnp.where(pick, line, 0.0), axis=1, keepdims=True)

    own_up, own_down = column(pack_ref[0:4, :]), column(pack_ref[4:8, :])
    for k in range(units // 128):
        cut = slice(k * 128, (k + 1) * 128)
        total = arrived_ref[0, :, cut].astype(f32)
        for p in range(1, peers):
            total += arrived_ref[p, :, cut].astype(f32)
        part = own_up * pack_ref[16 + k : 17 + k, :] - own_down * total
        grad_ref[:, cut] = part.astype(bf16)


def hidden_gradient(spot, arrived, pack):
    peers, rows, units = arrived.shape
    return pl.pallas_call(
        hidden_kernel,
        grid=(1,),
        in_specs=[pl.BlockSpec(memory_space=pltpu.SMEM), pl.BlockSpec(arrived.shape, lambda i: (0, 0, 0)), INSIDE],
        out_specs=INSIDE,
        out_shape=jax.ShapeDtypeStruct((rows, units), bf16),
        compiler_params=kernel_params(),
        cost_estimate=pl.CostEstimate(
            flops=4 * arrived.size, bytes_accessed=2 * arrived.size, transcendentals=0
        ),
        name="hidden_gradient",
    )(spot.reshape(1), arrived, pack)


def weight_kernel(
    own_pack_ref, other_pack_ref, own_ref, other_ref, scale_ref, hidden_ref, other_hidden_ref,
    out_ref, loss_ref, held_ref, rows_ref, result_ref, in_sems, out_sems,
):
    tokens, width = own_ref.shape
    parts, units = result_ref.shape[:2]
    sources = (hidden_ref, other_hidden_ref)

    def fetch(s):
        return pltpu.make_async_copy(sources[s], held_ref.at[s], in_sems.at[s])

    def send(j):
        part = out_ref.at[j * units : (j + 1) * units, :]
        return pltpu.make_async_copy(result_ref.at[j], part, out_sems.at[j])

    for s in range(2):
        fetch(s).start()
    loss_ref[0, 0] = jnp.max(own_pack_ref[12:13, :]) + jnp.max(other_pack_ref[12:13, :])
    packs = jnp.concatenate(
        [own_pack_ref[0:16, :], other_pack_ref[0:16, :], jnp.zeros((96, 128), f32)], axis=0
    )
    columns = jnp.transpose(packs)
    for s, part_ref in enumerate((own_ref, other_ref)):
        for r in range(tokens // 128):
            up = columns[:, 16 * s + r : 16 * s + r + 1]
            down = columns[:, 16 * s + 4 + r : 16 * s + 5 + r]
            part = part_ref[r * 128 : (r + 1) * 128, :].astype(f32)
            line = up * scale_ref[0:1, :] - down * part
            rows_ref[s * tokens + r * 128 : s * tokens + (r + 1) * 128, :] = line.astype(bf16)
    for s in range(2):
        fetch(s).wait()
    for j in range(parts):
        cut = slice(j * units, (j + 1) * units)
        result_ref[j] = lax.dot_general(
            held_ref[0, :, cut], rows_ref[:tokens, :], TN, preferred_element_type=f32
        ) + lax.dot_general(
            held_ref[1, :, cut], rows_ref[tokens:, :], TN, preferred_element_type=f32
        )
        send(j).start()
    for j in range(parts):
        send(j).wait()


def weight_gradient(own_pack, other_pack, own, other, scale, hidden, other_hidden):
    tokens, units = hidden.shape
    width = own.shape[1]
    parts = 2
    return pl.pallas_call(
        weight_kernel,
        in_specs=[INSIDE] * 5 + [OUTSIDE] * 2,
        out_specs=[pl.BlockSpec(memory_space=pltpu.HBM), pl.BlockSpec(memory_space=pltpu.SMEM)],
        out_shape=[pltpu.HBM((units, width), f32), jax.ShapeDtypeStruct((1, 1), f32)],
        scratch_shapes=[
            pltpu.VMEM((2, tokens, units), bf16),
            pltpu.VMEM((2 * tokens, width), bf16),
            pltpu.VMEM((parts, units // parts, width), f32),
            pltpu.SemaphoreType.DMA((2,)),
            pltpu.SemaphoreType.DMA((parts,)),
        ],
        compiler_params=kernel_params(),
        cost_estimate=pl.CostEstimate(
            flops=4 * units * tokens * width, bytes_accessed=8 * units * width, transcendentals=0
        ),
        name="weight_gradient",
    )(own_pack, other_pack, own, other, scale, hidden, other_hidden)


def place_of(yh, core, x, yl):
    return ((yh * 2 + core) * 4 + x) * 2 + yl


def lines(first):
    groups = []
    for core in range(2):
        if (core == 0) == first:
            groups += [[place_of(yh, core, x, yl) for x in range(4)] for yh in range(2) for yl in range(2)]
        else:
            groups += [[place_of(yh, core, x, yl) for yh in range(2) for yl in range(2)] for x in range(4)]
    return groups


def planes():
    along_y = [(yh, yl) for yh in range(2) for yl in range(2)]
    return [
        [place_of(yh, 0, x, yl) for yh, yl in along_y for x in range(4)],
        [place_of(yh, 1, x, yl) for x in range(4) for yh, yl in along_y],
    ]


def block_at(core, index):
    y = jnp.where(core == 0, index // 4, index % 4)
    x = jnp.where(core == 0, index % 4, index // 4)
    return y // 2, x * 2 + y % 2


def neighbours():
    pairs = [(z, z ^ 1) for z in range(16)]
    return pairs + [(16 + z, 16 + (z + (1 if z % 2 else -1)) % 16) for z in range(16)]


def on_device(
    hidden_act,
    down_weight,
    residual,
    head_weight,
    gain,
    behavior,
    frozen,
    old_values,
    judge_ratings,
    lengths,
):
    yh, core = lax.axis_index("yh"), lax.axis_index("core")
    parity = lax.axis_index("zl")
    z = 2 * lax.axis_index("zh") + parity
    x, y = lax.axis_index("x"), 2 * yh + lax.axis_index("yl")
    spot = jnp.where(core == 0, y * 4 + x, x * 4 + y)
    rows_each, units = hidden_act.shape
    width = down_weight.shape[1]
    chip = 2 * width
    group = 16 * rows_each
    section_rows = 8 * rows_each

    hidden = lax.all_to_all(
        spread(hidden_act, 4), SECTION, 0, 0, tiled=True, axis_index_groups=lines(True)
    ).reshape(4 * rows_each, units)
    far_weight = lax.ppermute(down_weight, "core", SWAP)
    hidden, far_weight, residual = lax.optimization_barrier((hidden, far_weight, residual))
    hidden = lax.all_to_all(
        spread(hidden, 4), SECTION, 0, 0, tiled=True, axis_index_groups=lines(False)
    ).reshape(16, rows_each, units)
    other_weight = hold(far_weight)

    chip_scale = lax.dynamic_slice_in_dim(gain * head_weight, yh * chip, chip, 0)
    own_scale = lax.dynamic_slice_in_dim(chip_scale, core * width, width, 0)
    other_scale = lax.dynamic_slice_in_dim(chip_scale, (1 - core) * width, width, 0)
    scale = jnp.concatenate([own_scale, other_scale])

    holder, phase = block_at(core, z)
    kept = lax.dynamic_slice_in_dim(residual, phase * rows_each, rows_each, 0)
    sent = lax.dynamic_slice_in_dim(kept, (1 - yh) * chip, chip, 1)
    mine = lax.dynamic_slice_in_dim(kept, yh * chip, chip, 1)
    stream = jnp.where(yh == holder, mine, lax.ppermute(sent, "yh", SWAP))
    left, right = stream[:, :width], stream[:, width:]
    stream = jnp.concatenate(
        [jnp.where(core == 0, left, right), jnp.where(core == 0, right, left)], axis=1
    )

    scale_rows = jnp.pad(jnp.stack(pieces(scale, 3)), ((0, 13), (0, 0))).astype(bf16)
    scale_back = lax.dot_general(
        scale_rows[:, :width], down_weight, NT, preferred_element_type=f32
    ) + lax.dot_general(scale_rows[:, width:], other_weight, NT, preferred_element_type=f32)
    base = jnp.sum(scale_back, axis=0).reshape(-1, 128)
    base = jnp.pad(base, ((0, 16 - base.shape[0]), (0, 0))).astype(bf16)
    slot = jnp.arange(group, dtype=jnp.int32)
    owner_yh, phase = block_at(core, slot // rows_each)
    token = (2 * owner_yh + core) * section_rows + phase * rows_each + slot % rows_each
    own_old, advantage = returns_of(behavior, frozen, old_values, judge_ratings, lengths, token)
    returns = own_old + advantage
    returns, own_old = returns.reshape(4, 128), own_old.reshape(4, 128)
    hidden, returns, own_old, other_weight = lax.optimization_barrier(
        (hidden, returns, own_old, other_weight)
    )

    away = forward(hidden, down_weight, other_weight, 1 - parity, bf16)
    met = lax.ppermute(away, ("core", "zh", "zl"), neighbours())
    kept_half = forward(hidden, down_weight, other_weight, parity, f32)
    hidden, kept_half = lax.optimization_barrier((hidden.reshape(group, units), kept_half))
    far_hidden = lax.ppermute(hidden, "core", SWAP)
    pair = (kept_half + met.astype(f32)).astype(bf16)
    parts = lax.all_to_all(pair.reshape(8, rows_each, chip), "zh", 0, 0, tiled=True)
    combined = (jnp.sum(parts.astype(f32), axis=0) + stream.astype(f32)).astype(bf16)
    combined = lax.all_gather(combined, ("zh", "zl"), axis=0, tiled=True)
    own_columns, other_columns = combined[:, :width], combined[:, width:]

    sums = token_sums(combined, scale_rows, base, 16)
    sums = lax.all_to_all(sums, SECTION, 0, 0, tiled=True, axis_index_groups=planes())
    payload = back(combined, down_weight, other_weight, 16)
    sums, payload = lax.optimization_barrier((sums, payload))
    arrived = lax.all_to_all(payload, SECTION, 0, 0, tiled=True, axis_index_groups=planes())
    far_columns = lax.ppermute(other_columns, "core", SWAP)
    pack = token_terms(sums, own_old, returns, combined)
    hidden_grad = hidden_gradient(spot, arrived, pack)
    other_pack = lax.ppermute(pack, "core", SWAP)
    weight_grad, total_loss = weight_gradient(
        pack, other_pack, own_columns, far_columns, own_scale.reshape(1, -1), hidden, far_hidden
    )
    own_head = pack[8:10] + other_pack[10:12]
    other_head = pack[10:12] + other_pack[8:10]
    head_chip = jnp.concatenate(
        [jnp.where(core == 0, own_head, other_head), jnp.where(core == 0, other_head, own_head)]
    )
    head_far = lax.ppermute(head_chip, "yh", SWAP)
    head_far, total_loss = lax.optimization_barrier((head_far, total_loss))
    head_sum = jnp.concatenate(
        [jnp.where(yh == 0, head_chip, head_far), jnp.where(yh == 0, head_far, head_chip)]
    )
    head_grad = gain * head_sum.reshape(-1)
    return (total_loss[0, 0], head_grad, weight_grad, hidden_grad)


def solution(mesh):
    axes = ("yh", "core", "x", "yl", "zh", "zl")
    fine = Mesh(mesh.devices.reshape(2, 2, 4, 2, 8, 2), axes)
    tp = ("zh", "zl")
    in_specs = (
        P(("yh", "core", "x", "yl"), tp),
        P(tp, ("x", "yl", "yh", "core")),
        P(("yh", "core"), ("x", "yl")),
        P(("x", "yl")),
        P(("x", "yl")),
        P(),
        P(),
        P(),
        P(),
        P(),
    )
    out_specs = (
        P(),
        P(("x", "yl")),
        P(tp, ("x", "yl", "yh", "core")),
        P(("yh", "core", "x", "yl"), tp),
    )
    return jax.shard_map(
        on_device, mesh=fine, in_specs=in_specs, out_specs=out_specs, check_vma=False
    )
```

```python
import jax
import jax.numpy as jnp
from jax import lax
from jax.experimental import pallas as pl
from jax.experimental.pallas import tpu as pltpu
from jax.sharding import Mesh, PartitionSpec as P

D = 8192
KL_PENALTY_SCALE = 0.1
TRACE_DECAY = 0.95
CLIP_RANGE = 0.2
EPSILON = 1e-05

SECTION = ("yh", "core", "x", "yl")
SWAP = [(0, 1), (1, 0)]
f32, bf16 = jnp.float32, jnp.bfloat16


def returns_of(behavior, frozen, old_values, judge_ratings, lengths, rows):
    total = behavior.shape[0]
    position = jnp.arange(total, dtype=jnp.int32)
    ends = jnp.cumsum(lengths)
    closes = position[:, None] == ends[None, :] - 1
    final = jnp.any(closes, axis=1)
    extra = jnp.sum(jnp.where(closes, judge_ratings[None, :], 0.0), axis=1)
    rewards = extra - KL_PENALTY_SCALE * (behavior - frozen)
    following = jnp.concatenate([old_values[1:], jnp.zeros_like(old_values[:1])])
    delta = rewards + jnp.where(final, 0.0, following) - old_values
    segment = jnp.sum((position[:, None] >= ends[None, :]).astype(jnp.int32), axis=1)
    row_seg = jnp.sum((rows[:, None] >= ends[None, :]).astype(jnp.int32), axis=1)
    gap = position[None, :] - rows[:, None]
    inside = (row_seg[:, None] == segment[None, :]) & (gap >= 0)
    powers = jnp.power(jnp.float32(TRACE_DECAY), jnp.maximum(gap, 0).astype(f32))
    here = jnp.sum(jnp.where(gap == 0, old_values[None, :], 0.0), axis=1)
    return here, jnp.sum(jnp.where(inside, powers, 0.0) * delta[None, :], axis=1)


def pieces(x, count):
    out = []
    for _ in range(count):
        top = lax.reduce_precision(x, 8, 7)
        out.append(top)
        x = x - top
    return out


def kernel_params():
    return pltpu.CompilerParams(vmem_limit_bytes=16 * 1024 * 1024)


NT = (((1,), (1,)), ((), ()))
TN = (((0,), (0,)), ((), ()))
INSIDE = pl.BlockSpec(memory_space=pltpu.VMEM)
OUTSIDE = pl.BlockSpec(memory_space=pl.ANY)


def near(*arrays):
    return [pltpu.with_memory_space_constraint(a, pltpu.VMEM) for a in arrays]


def far(array):
    return pltpu.with_memory_space_constraint(array, pltpu.HBM)


def hold_kernel(in_ref, out_ref, sem):
    copy = pltpu.make_async_copy(in_ref, out_ref, sem)
    copy.start()
    copy.wait()


def hold(x):
    return pl.pallas_call(
        hold_kernel,
        in_specs=[pl.BlockSpec(memory_space=pl.ANY)],
        out_specs=INSIDE,
        out_shape=pltpu.VMEM(x.shape, x.dtype),
        scratch_shapes=[pltpu.SemaphoreType.DMA],
        compiler_params=kernel_params(),
        cost_estimate=pl.CostEstimate(flops=0, bytes_accessed=4 * x.size, transcendentals=0),
        name="hold",
    )(x)


def spread_kernel(in_ref, out_ref, held_ref, sem, sems):
    first = pltpu.make_async_copy(in_ref, held_ref, sem)
    first.start()
    first.wait()
    copies = [
        pltpu.make_async_copy(held_ref, out_ref.at[i], sems.at[i]) for i in range(out_ref.shape[0])
    ]
    for copy in copies:
        copy.start()
    for copy in copies:
        copy.wait()


def spread(x, count):
    return pl.pallas_call(
        spread_kernel,
        in_specs=[pl.BlockSpec(memory_space=pl.ANY)],
        out_specs=pl.BlockSpec(memory_space=pltpu.HBM),
        out_shape=pltpu.HBM((count,) + x.shape, x.dtype),
        scratch_shapes=[
            pltpu.VMEM(x.shape, x.dtype),
            pltpu.SemaphoreType.DMA,
            pltpu.SemaphoreType.DMA((count,)),
        ],
        compiler_params=kernel_params(),
        cost_estimate=pl.CostEstimate(flops=0, bytes_accessed=2 * count * x.size, transcendentals=0),
        name="spread",
    )(x)


def forward_kernel(half_ref, hidden_ref, own_ref, other_ref, out_ref):
    half = hidden_ref[:, pl.ds(half_ref[0], 1)]
    rows = half.reshape(out_ref.shape[0], hidden_ref.shape[-1])
    width = own_ref.shape[1]
    for i, w_ref in enumerate((own_ref, other_ref)):
        product = jnp.dot(rows, w_ref[...], preferred_element_type=f32)
        out_ref[:, i * width : (i + 1) * width] = product.astype(out_ref.dtype)


def forward(hidden, own_weight, other_weight, half, dtype):
    count, rows, units = hidden.shape
    width = own_weight.shape[1]
    tokens = count // 2 * rows
    return pl.pallas_call(
        forward_kernel,
        in_specs=[pl.BlockSpec(memory_space=pltpu.SMEM)] + [INSIDE] * 3,
        out_specs=INSIDE,
        out_shape=jax.ShapeDtypeStruct((tokens, 2 * width), dtype),
        compiler_params=kernel_params(),
        cost_estimate=pl.CostEstimate(
            flops=4 * tokens * units * width, bytes_accessed=4 * units * width, transcendentals=0
        ),
        name="forward",
    )(half.reshape(1), *near(hidden.reshape(count // 2, 2, rows, units), own_weight, other_weight))


def sums_kernel(combined_ref, scale_ref, base_ref, out_ref, held_ref, rows_ref, sem):
    peers, rows, lanes = out_ref.shape
    both = combined_ref[...]
    wide = both.astype(f32)
    square = wide * wide
    top = square.astype(bf16)
    rest = (square - top.astype(f32)).astype(bf16)
    ones = jnp.ones((16, both.shape[1]), bf16)
    squares = lax.dot_general(ones, top, NT, preferred_element_type=f32)
    squares += lax.dot_general(ones, rest, NT, preferred_element_type=f32)
    products = lax.dot_general(scale_ref[...], both, NT, preferred_element_type=f32)
    place = 0
    for line in (squares[0:1], jnp.sum(products, axis=0, keepdims=True)):
        top = line.astype(bf16).astype(f32)
        for part in (top, line - top):
            for i in range(4):
                rows_ref[place : place + 1, :] = part[:, i * lanes : (i + 1) * lanes]
                place += 1
    sums = rows_ref[...].astype(bf16)
    held_ref[:, :16, :] = jnp.broadcast_to(sums[None], (peers, 16, lanes))
    held_ref[:, 16:, :] = jnp.broadcast_to(base_ref[...][None], (peers, rows - 16, lanes))
    copy = pltpu.make_async_copy(held_ref, out_ref, sem)
    copy.start()
    copy.wait()


def token_sums(combined, scale_rows, base, peers):
    shape = (peers, 32, 128)
    return pl.pallas_call(
        sums_kernel,
        in_specs=[INSIDE] * 3,
        out_specs=pl.BlockSpec(memory_space=pltpu.HBM),
        out_shape=pltpu.HBM(shape, bf16),
        scratch_shapes=[pltpu.VMEM(shape, bf16), pltpu.VMEM((16, 128), f32), pltpu.SemaphoreType.DMA],
        compiler_params=kernel_params(),
        cost_estimate=pl.CostEstimate(flops=96 * combined.size, bytes_accessed=2 * combined.size, transcendentals=0),
        name="token_sums",
    )(*near(combined), scale_rows, base)


def back_kernel(combined_ref, outer_ref, other_ref, out_ref, own_ref, held_ref, sem, sems):
    copy = pltpu.make_async_copy(outer_ref, own_ref, sem)
    copy.start()
    width = own_ref.shape[1]
    parts, peers, rows, lanes = held_ref.shape

    def send(j):
        target = out_ref.at[:, :, j * lanes : (j + 1) * lanes]
        return pltpu.make_async_copy(held_ref.at[j], target, sems.at[j])

    for j in range(parts):
        cut = slice(j * lanes, (j + 1) * lanes)
        total = lax.dot_general(
            combined_ref[:, width:], other_ref[cut, :], NT, preferred_element_type=f32
        )
        if j == 0:
            copy.wait()
        total += lax.dot_general(
            combined_ref[:, :width], own_ref[cut, :], NT, preferred_element_type=f32
        )
        held_ref[j] = total.astype(bf16).reshape(peers, rows, lanes)
        send(j).start()
    for j in range(parts):
        send(j).wait()


def back(combined, own_weight, other_weight, peers):
    tokens, chip = combined.shape
    units, width = own_weight.shape
    rows, parts = tokens // peers, 2
    return pl.pallas_call(
        back_kernel,
        in_specs=[INSIDE, OUTSIDE, INSIDE],
        out_specs=pl.BlockSpec(memory_space=pltpu.HBM),
        out_shape=pltpu.HBM((peers, rows, units), bf16),
        scratch_shapes=[
            pltpu.VMEM((units, width), bf16),
            pltpu.VMEM((parts, peers, rows, units // parts), bf16),
            pltpu.SemaphoreType.DMA,
            pltpu.SemaphoreType.DMA((parts,)),
        ],
        compiler_params=kernel_params(),
        cost_estimate=pl.CostEstimate(
            flops=4 * tokens * units * width, bytes_accessed=8 * units * width, transcendentals=0
        ),
        name="back",
    )(*near(combined), far(own_weight), *near(other_weight))


def token_kernel(sums_ref, old_ref, returns_ref, combined_ref, pack_ref, up_ref):
    sums = jnp.sum(sums_ref[...].astype(f32), axis=0)
    square_sum = sums[0:4] + sums[4:8]
    product_sum = sums[8:12] + sums[12:16]
    pack_ref[16:32, :] = sums[16:32]
    old, returns = old_ref[...], returns_ref[...]
    rinv = lax.rsqrt(square_sum / D + EPSILON)
    values = rinv * product_sum
    squash = jnp.tanh((values - old) / CLIP_RANGE)
    clipped = old + CLIP_RANGE * squash
    first = (values - returns) ** 2
    second = (clipped - returns) ** 2
    loss = 0.25 * jnp.sum(first + second)
    dvalue = 0.5 * (values - returns) + 0.5 * (clipped - returns) * (1.0 - squash * squash)
    up = dvalue * rinv
    down = up * rinv * values / D
    pack_ref[0:4, :] = up
    pack_ref[4:8, :] = down
    pack_ref[12:16, :] = jnp.full((4, 128), loss, f32)

    up_ref[...] = jnp.zeros_like(up_ref)
    rest = up
    for i in range(3):
        top = rest.astype(bf16).astype(f32)
        rest = rest - top
        for r in range(4):
            up_ref[i : i + 1, r * 128 : (r + 1) * 128] = top[r : r + 1, :]
    head = jnp.dot(up_ref[...].astype(bf16), combined_ref[...], preferred_element_type=f32)
    head = jnp.sum(head, axis=0, keepdims=True)
    for r in range(4):
        pack_ref[8 + r : 9 + r, :] = head[:, r * 128 : (r + 1) * 128]


def token_terms(sums, old, returns, combined):
    return pl.pallas_call(
        token_kernel,
        in_specs=[INSIDE] * 4,
        out_specs=INSIDE,
        out_shape=jax.ShapeDtypeStruct((32, 128), f32),
        scratch_shapes=[pltpu.VMEM((16, combined.shape[0]), f32)],
        compiler_params=kernel_params(),
        cost_estimate=pl.CostEstimate(flops=4 * combined.size, bytes_accessed=2 * combined.size, transcendentals=0),
        name="token_terms",
    )(sums, old, returns, combined)


def hidden_kernel(spot_ref, arrived_ref, pack_ref, grad_ref):
    spot = spot_ref[0]
    peers, rows, units = arrived_ref.shape
    which = lax.broadcasted_iota(jnp.int32, (4, 128), 0) == spot // 4
    lane = lax.broadcasted_iota(jnp.int32, (rows, 128), 1)
    sub = lax.broadcasted_iota(jnp.int32, (rows, 128), 0)
    pick = lane == sub + lax.rem(spot, 4) * rows

    def column(x):
        line = jnp.sum(jnp.where(which, x, 0.0), axis=0, keepdims=True)
        return jnp.sum(jnp.where(pick, line, 0.0), axis=1, keepdims=True)

    own_up, own_down = column(pack_ref[0:4, :]), column(pack_ref[4:8, :])
    for k in range(units // 128):
        cut = slice(k * 128, (k + 1) * 128)
        total = arrived_ref[0, :, cut].astype(f32)
        for p in range(1, peers):
            total += arrived_ref[p, :, cut].astype(f32)
        part = own_up * pack_ref[16 + k : 17 + k, :] - own_down * total
        grad_ref[:, cut] = part.astype(bf16)


def hidden_gradient(spot, arrived, pack):
    peers, rows, units = arrived.shape
    return pl.pallas_call(
        hidden_kernel,
        grid=(1,),
        in_specs=[pl.BlockSpec(memory_space=pltpu.SMEM), pl.BlockSpec(arrived.shape, lambda i: (0, 0, 0)), INSIDE],
        out_specs=INSIDE,
        out_shape=jax.ShapeDtypeStruct((rows, units), bf16),
        compiler_params=kernel_params(),
        cost_estimate=pl.CostEstimate(
            flops=4 * arrived.size, bytes_accessed=2 * arrived.size, transcendentals=0
        ),
        name="hidden_gradient",
    )(spot.reshape(1), arrived, pack)


def weight_kernel(
    own_pack_ref, other_pack_ref, own_ref, other_ref, scale_ref, hidden_ref, other_hidden_ref,
    out_ref, loss_ref, held_ref, rows_ref, result_ref, in_sems, out_sems,
):
    tokens, width = own_ref.shape
    parts, units = result_ref.shape[:2]
    sources = (hidden_ref, other_hidden_ref)

    def fetch(s):
        return pltpu.make_async_copy(sources[s], held_ref.at[s], in_sems.at[s])

    def send(j):
        part = out_ref.at[j * units : (j + 1) * units, :]
        return pltpu.make_async_copy(result_ref.at[j], part, out_sems.at[j])

    for s in range(2):
        fetch(s).start()
    loss_ref[0, 0] = jnp.max(own_pack_ref[12:13, :]) + jnp.max(other_pack_ref[12:13, :])
    packs = jnp.concatenate(
        [own_pack_ref[0:16, :], other_pack_ref[0:16, :], jnp.zeros((96, 128), f32)], axis=0
    )
    columns = jnp.transpose(packs)
    for s, part_ref in enumerate((own_ref, other_ref)):
        for r in range(tokens // 128):
            up = columns[:, 16 * s + r : 16 * s + r + 1]
            down = columns[:, 16 * s + 4 + r : 16 * s + 5 + r]
            part = part_ref[r * 128 : (r + 1) * 128, :].astype(f32)
            line = up * scale_ref[0:1, :] - down * part
            rows_ref[s * tokens + r * 128 : s * tokens + (r + 1) * 128, :] = line.astype(bf16)
    for s in range(2):
        fetch(s).wait()
    for j in range(parts):
        cut = slice(j * units, (j + 1) * units)
        result_ref[j] = lax.dot_general(
            held_ref[0, :, cut], rows_ref[:tokens, :], TN, preferred_element_type=f32
        ) + lax.dot_general(
            held_ref[1, :, cut], rows_ref[tokens:, :], TN, preferred_element_type=f32
        )
        send(j).start()
    for j in range(parts):
        send(j).wait()


def weight_gradient(own_pack, other_pack, own, other, scale, hidden, other_hidden):
    tokens, units = hidden.shape
    width = own.shape[1]
    parts = 2
    return pl.pallas_call(
        weight_kernel,
        in_specs=[INSIDE] * 5 + [OUTSIDE] * 2,
        out_specs=[pl.BlockSpec(memory_space=pltpu.HBM), pl.BlockSpec(memory_space=pltpu.SMEM)],
        out_shape=[pltpu.HBM((units, width), f32), jax.ShapeDtypeStruct((1, 1), f32)],
        scratch_shapes=[
            pltpu.VMEM((2, tokens, units), bf16),
            pltpu.VMEM((2 * tokens, width), bf16),
            pltpu.VMEM((parts, units // parts, width), f32),
            pltpu.SemaphoreType.DMA((2,)),
            pltpu.SemaphoreType.DMA((parts,)),
        ],
        compiler_params=kernel_params(),
        cost_estimate=pl.CostEstimate(
            flops=4 * units * tokens * width, bytes_accessed=8 * units * width, transcendentals=0
        ),
        name="weight_gradient",
    )(own_pack, other_pack, own, other, scale, hidden, other_hidden)


def place_of(yh, core, x, yl):
    return ((yh * 2 + core) * 4 + x) * 2 + yl


def lines(first):
    groups = []
    for core in range(2):
        if (core == 0) == first:
            groups += [[place_of(yh, core, x, yl) for x in range(4)] for yh in range(2) for yl in range(2)]
        else:
            groups += [[place_of(yh, core, x, yl) for yh in range(2) for yl in range(2)] for x in range(4)]
    return groups


def planes():
    along_y = [(yh, yl) for yh in range(2) for yl in range(2)]
    return [
        [place_of(yh, 0, x, yl) for yh, yl in along_y for x in range(4)],
        [place_of(yh, 1, x, yl) for x in range(4) for yh, yl in along_y],
    ]


def block_at(core, index):
    y = jnp.where(core == 0, index // 4, index % 4)
    x = jnp.where(core == 0, index % 4, index // 4)
    return y // 2, x * 2 + y % 2


def neighbours():
    pairs = [(z, z ^ 1) for z in range(16)]
    return pairs + [(16 + z, 16 + (z + (1 if z % 2 else -1)) % 16) for z in range(16)]


def on_device(
    hidden_act,
    down_weight,
    residual,
    head_weight,
    gain,
    behavior,
    frozen,
    old_values,
    judge_ratings,
    lengths,
):
    yh, core = lax.axis_index("yh"), lax.axis_index("core")
    parity = lax.axis_index("zl")
    z = 2 * lax.axis_index("zh") + parity
    x, y = lax.axis_index("x"), 2 * yh + lax.axis_index("yl")
    spot = jnp.where(core == 0, y * 4 + x, x * 4 + y)
    rows_each, units = hidden_act.shape
    width = down_weight.shape[1]
    chip = 2 * width
    group = 16 * rows_each
    section_rows = 8 * rows_each

    hidden = lax.all_to_all(
        spread(hidden_act, 4), SECTION, 0, 0, tiled=True, axis_index_groups=lines(True)
    ).reshape(4 * rows_each, units)
    hidden, moved_weight, residual, old_values = lax.optimization_barrier(
        (hidden, down_weight, residual, old_values)
    )
    hidden = lax.all_to_all(
        spread(hidden, 4), SECTION, 0, 0, tiled=True, axis_index_groups=lines(False)
    ).reshape(16, rows_each, units)
    other_weight = hold(lax.ppermute(moved_weight, "core", SWAP))

    chip_scale = lax.dynamic_slice_in_dim(gain * head_weight, yh * chip, chip, 0)
    own_scale = lax.dynamic_slice_in_dim(chip_scale, core * width, width, 0)
    other_scale = lax.dynamic_slice_in_dim(chip_scale, (1 - core) * width, width, 0)
    scale = jnp.concatenate([own_scale, other_scale])

    holder, phase = block_at(core, z)
    kept = lax.dynamic_slice_in_dim(residual, phase * rows_each, rows_each, 0)
    sent = lax.dynamic_slice_in_dim(kept, (1 - yh) * chip, chip, 1)
    mine = lax.dynamic_slice_in_dim(kept, yh * chip, chip, 1)
    stream = jnp.where(yh == holder, mine, lax.ppermute(sent, "yh", SWAP))
    left, right = stream[:, :width], stream[:, width:]
    stream = jnp.concatenate(
        [jnp.where(core == 0, left, right), jnp.where(core == 0, right, left)], axis=1
    )

    scale_rows = jnp.pad(jnp.stack(pieces(scale, 3)), ((0, 13), (0, 0))).astype(bf16)
    scale_back = lax.dot_general(
        scale_rows[:, :width], down_weight, NT, preferred_element_type=f32
    ) + lax.dot_general(scale_rows[:, width:], other_weight, NT, preferred_element_type=f32)
    base = jnp.sum(scale_back, axis=0).reshape(-1, 128)
    base = jnp.pad(base, ((0, 16 - base.shape[0]), (0, 0))).astype(bf16)
    slot = jnp.arange(group, dtype=jnp.int32)
    owner_yh, phase = block_at(core, slot // rows_each)
    token = (2 * owner_yh + core) * section_rows + phase * rows_each + slot % rows_each
    own_old, advantage = returns_of(behavior, frozen, old_values, judge_ratings, lengths, token)
    returns = own_old + advantage
    returns, own_old = returns.reshape(4, 128), own_old.reshape(4, 128)
    hidden, returns, own_old, other_weight = lax.optimization_barrier(
        (hidden, returns, own_old, other_weight)
    )

    away = forward(hidden, down_weight, other_weight, 1 - parity, bf16)
    met = lax.ppermute(away, ("core", "zh", "zl"), neighbours())
    kept_half = forward(hidden, down_weight, other_weight, parity, f32)
    hidden, kept_half = lax.optimization_barrier((hidden.reshape(group, units), kept_half))
    far_hidden = lax.ppermute(hidden, "core", SWAP)
    pair = (kept_half + met.astype(f32)).astype(bf16)
    parts = lax.all_to_all(pair.reshape(8, rows_each, chip), "zh", 0, 0, tiled=True)
    combined = (jnp.sum(parts.astype(f32), axis=0) + stream.astype(f32)).astype(bf16)
    combined = lax.all_gather(combined, ("zh", "zl"), axis=0, tiled=True)
    own_columns, other_columns = combined[:, :width], combined[:, width:]

    sums = token_sums(combined, scale_rows, base, 16)
    sums = lax.all_to_all(sums, SECTION, 0, 0, tiled=True, axis_index_groups=planes())
    payload = back(combined, down_weight, other_weight, 16)
    sums, payload = lax.optimization_barrier((sums, payload))
    arrived = lax.all_to_all(payload, SECTION, 0, 0, tiled=True, axis_index_groups=planes())
    far_columns = lax.ppermute(other_columns, "core", SWAP)
    pack = token_terms(sums, own_old, returns, combined)
    hidden_grad = hidden_gradient(spot, arrived, pack)
    other_pack = lax.ppermute(pack, "core", SWAP)
    weight_grad, total_loss = weight_gradient(
        pack, other_pack, own_columns, far_columns, own_scale.reshape(1, -1), hidden, far_hidden
    )
    own_head = pack[8:10] + other_pack[10:12]
    other_head = pack[10:12] + other_pack[8:10]
    head_chip = jnp.concatenate(
        [jnp.where(core == 0, own_head, other_head), jnp.where(core == 0, other_head, own_head)]
    )
    head_far = lax.ppermute(head_chip, "yh", SWAP)
    head_far, total_loss = lax.optimization_barrier((head_far, total_loss))
    head_sum = jnp.concatenate(
        [jnp.where(yh == 0, head_chip, head_far), jnp.where(yh == 0, head_far, head_chip)]
    )
    head_grad = gain * head_sum.reshape(-1)
    return (total_loss[0, 0], head_grad, weight_grad, hidden_grad)


def solution(mesh):
    axes = ("yh", "core", "x", "yl", "zh", "zl")
    fine = Mesh(mesh.devices.reshape(2, 2, 4, 2, 8, 2), axes)
    tp = ("zh", "zl")
    in_specs = (
        P(("yh", "core", "x", "yl"), tp),
        P(tp, ("x", "yl", "yh", "core")),
        P(("yh", "core"), ("x", "yl")),
        P(("x", "yl")),
        P(("x", "yl")),
        P(),
        P(),
        P(),
        P(),
        P(),
    )
    out_specs = (
        P(),
        P(("x", "yl")),
        P(tp, ("x", "yl", "yh", "core")),
        P(("yh", "core", "x", "yl"), tp),
    )
    return jax.shard_map(
        on_device, mesh=fine, in_specs=in_specs, out_specs=out_specs, check_vma=False
    )
```
